128 devices in a mesh: blk: 32 (over x, y, core), wid: 4 (over z).
Axes of the slice: x: 4, y: 4, z: 4, core: 2. Of those that a mesh axis runs over, the one named last changes fastest.
Arguments:
- queries: bfloat16 [7168, 4096], P('blk', 'wid'), may hold values from -30 to 30
- passages: bfloat16 [7168, 4096], P('blk', 'wid'), may hold values from -7 to 7
- pairs: int32 [32, 32], replicated, may hold values from 0 to 1, as said below
Outputs:
- loss: float32 [], replicated
- grad_queries: bfloat16 [7168, 4096], P('blk', 'wid')
- grad_passages: bfloat16 [7168, 4096], P('blk', 'wid')
The draws below stay inside these ranges and needn't reach their ends.
Inputs may be any that keep to these rules, and one draw needn't show every extreme that they name: pairs is 0 on its diagonal; each query block lists its own number of hard-negative blocks, each at most once.
All inputs are finite; a program needn't handle non-finite values.
Results may differ from the reference program's by a relative error of at most 0.017.
Values may be sent and summed in bfloat16 or wider, within the bound.
A program may use at most 128 MiB of HBM per device.

```python
import jax
import jax.numpy as jnp
from jax import lax

D = 4096
BR = 224
N_BLK = 32


def passage_base(key):
    values = jax.random.normal(jax.random.fold_in(key, 101), (N_BLK * BR, D), jnp.float32)
    return jnp.clip(values, -6.0, 6.0)


def block_place():
    row_ids = jnp.arange(N_BLK * BR, dtype=jnp.int32)
    return ((row_ids // BR).astype(jnp.float32) / max(N_BLK - 1, 1))[:, None]


def block_growth(power):
    return (1.0 + 3.0 * block_place()) ** power


def draw_passages(key, part):
    base = passage_base(key)
    return base.astype(jnp.bfloat16)


def draw_queries(key, part):
    base = passage_base(key)
    key = jax.random.fold_in(key, 7)
    values = jnp.clip(jax.random.normal(key, (N_BLK * BR, D), jnp.float32), -6.0, 6.0) * block_growth(1.0)
    values = values + 0.15 * (1.0 - block_place()) * base
    return values.astype(jnp.bfloat16)


def draw_pairs(key, part):
    key = jax.random.fold_in(key, 3)
    limits = jax.random.randint(jax.random.fold_in(key, 1), (N_BLK, 1), 10, 90)
    rolls = jax.random.randint(jax.random.fold_in(key, 2), (N_BLK, N_BLK), 0, 100)
    ids = jnp.arange(N_BLK, dtype=jnp.int32)
    chosen = (rolls < limits) & (ids[:, None] != ids[None, :])
    return jnp.where(chosen, 1, 0).astype(jnp.int32)


def setup_inputs(seed: int = 0) -> dict:
    arg_keys = jax.random.split(jax.random.key(seed), 4)
    return {
        "queries": draw_queries(jax.random.fold_in(arg_keys[3], 71), 0),
        "passages": draw_passages(jax.random.fold_in(arg_keys[3], 71), 0),
        "pairs": draw_pairs(jax.random.fold_in(arg_keys[3], 71), 0),
    }


def softmax_weights(scores, colmask, pos_cols):
    masked = jnp.where(colmask[None, :], scores, -jnp.inf)
    highest = jnp.max(masked, axis=1, keepdims=True)
    expon = jnp.exp(masked - highest)
    totals = jnp.sum(expon, axis=1, keepdims=True)
    log_total = highest[:, 0] + jnp.log(totals[:, 0])
    onehot = jnp.arange(scores.shape[1], dtype=jnp.int32)[None, :] == pos_cols[:, None]
    positive = jnp.sum(jnp.where(onehot, scores, 0.0), axis=1)
    prob = expon / totals
    weights = (prob - onehot.astype(jnp.float32)).astype(jnp.bfloat16)
    return weights, jnp.sum(log_total - positive)


def reference(queries, passages, pairs):
    score_scale = D ** -0.5
    blocks = N_BLK
    col_block = jnp.arange(blocks * BR, dtype=jnp.int32) // BR

    def one_block(totals, index):
        query_rows = lax.dynamic_slice_in_dim(queries, (index * BR).astype(jnp.int32), BR, 0)
        pair_row = lax.dynamic_slice_in_dim(pairs, index.astype(jnp.int32), 1, 0)[0]
        allowed = (pair_row == 1) | (jnp.arange(blocks, dtype=jnp.int32) == index)
        colmask = allowed[col_block]
        scores = lax.dot_general(query_rows, passages, (((1,), (1,)), ((), ())), preferred_element_type=jnp.float32) * score_scale
        pos_cols = (index * BR + jnp.arange(BR, dtype=jnp.int32)).astype(jnp.int32)
        weights, loss_sum = softmax_weights(scores, colmask, pos_cols)
        grad_rows = jnp.dot(weights, passages, preferred_element_type=jnp.float32).astype(jnp.bfloat16)
        partial_term = lax.dot_general(weights, query_rows, (((0,), (0,)), ((), ())), preferred_element_type=jnp.float32)
        partial_term = lax.optimization_barrier(partial_term.astype(jnp.bfloat16)).astype(jnp.float32)
        return (totals[0] + partial_term, totals[1] + loss_sum), grad_rows

    start_totals = (jnp.zeros((blocks * BR, D), jnp.float32), jnp.zeros((), jnp.float32))
    (grad_sum, loss_sum), grad_rows = lax.scan(one_block, start_totals, jnp.arange(blocks, dtype=jnp.int32))
    loss = loss_sum / (blocks * BR)
    return loss, grad_rows.reshape(blocks * BR, D), grad_sum.astype(jnp.bfloat16)
```

```python
import jax
import jax.numpy as jnp
from jax import lax
from jax.experimental import pallas as pl
from jax.experimental.pallas import tpu as pltpu
from jax.sharding import PartitionSpec as P

MESH = pl.DeviceIdType.MESH
BR = 224
HALF = BR // 2
WC = 512
TILE = 4 * BR
CORE = 2 * BR
SUB = 32
NEG = -1e30
SCALE = 4096 ** -0.5
ORDER_IN = ((0, 1, 3, 2), (0, 3, 1, 2))
ORDER_OUT = ((2, 1, 3, 0), (2, 3, 1, 0))
F32 = jnp.float32
BF16 = jnp.bfloat16


def rows(slot, n=BR, off=0):
    return pl.ds(pl.multiple_of(slot * BR + off, 16), n)


def kernel(
    q_hbm, p_hbm, pairs_ref, loss_ref, gq_ref, gp_ref,
    qg, pg, tile, tile_in, wp, wq, st_f, in_f, st_n, in_n, st_z, in_z, stat, stats, lossv, losses,
    r1, s1, rn, sn, rf, sf, rt, sst, rst, sstat, rw, sw, rf5, sf5, rn5, sn5, rz, sz, rl, sl,
):
    blk = lax.axis_index("blk")
    z = lax.axis_index("wid")
    x = blk // 8
    y = (blk // 2) % 4
    c = blk % 2
    h = z // 2
    l = ((z + 1) // 2) % 2
    twin = h * 2 + (z + 1) % 2
    flip = 3 - z
    far_x, far_y = (x + 2) % 4, (y + 2) % 4

    def dev(xx, yy, cc, zz):
        return ((xx * 4 + yy) * 2 + cc, zz)

    right = (dev(x, (y + 1) % 4, c, z), dev((x + 1) % 4, y, c, z))
    left = (dev(x, (y + 3) % 4, c, z), dev((x + 3) % 4, y, c, z))
    other = dev(x, y, 1 - c, z)
    gathered = (qg, pg)
    pos = (y, x)

    def remote(src, dst, ssem, rsem, device):
        return pltpu.make_async_remote_copy(
            src_ref=src, dst_ref=dst, send_sem=ssem, recv_sem=rsem, device_id=device, device_id_type=MESH
        )

    def arrived(dst, sem):
        pltpu.make_async_copy(dst, dst, sem).wait()

    barrier = pltpu.get_barrier_semaphore()
    peers = [other]
    for dz in (1, 2, 3):
        for cc in (0, 1):
            peers.append(dev(x, y, cc, (z + dz) % 4))
    stat_peers = [other, dev(x, y, c, twin), dev(x, y, 1 - c, twin)]
    for dy in (1, 2, 3):
        for cc in (0, 1):
            for zz in (z, twin):
                peers.append(dev(x, (y + dy) % 4, cc, zz))
                stat_peers.append(peers[-1])
    loss_peers = [dev(x, y, c, flip)]
    for dx in (1, 2, 3):
        for zz in (z, flip):
            peers.append(dev((x + dx) % 4, y, c, zz))
            loss_peers.append(peers[-1])
    for peer in peers:
        pl.semaphore_signal(barrier, inc=1, device_id=peer, device_id_type=MESH)
    pl.semaphore_wait(barrier, len(peers))

    def along_z(start):
        for step in range(4):
            for which in (0, 1):
                d = ORDER_IN[which][step]
                zt = (z + 4 - d) % 4
                owner = zt // 2 if which == 0 else ((zt + 1) // 2) % 2

                @pl.when(owner == c)
                def _():
                    for part in (0, 1):
                        src = (q_hbm, p_hbm)[which].at[:, part * WC:(part + 1) * WC]
                        dst = gathered[which].at[d, rows(pos[which])]
                        copy = remote(src, dst, s1.at[which, d, part], r1.at[which, d], dev(x, y, part, zt))
                        if d == 0:
                            if start:
                                @pl.when(c == part)
                                def _():
                                    pltpu.make_async_copy(src, dst, r1.at[which, d]).start()

                            @pl.when(c != part)
                            def _():
                                copy.start() if start else copy.wait_send()
                        else:
                            copy.start() if start else copy.wait_send()

    along_z(True)

    def to_next(step, start):
        for which in (0, 1):
            d = ORDER_IN[which][step]
            own = gathered[which].at[d, rows(pos[which])]
            if start:
                arrived(own, r1.at[which, d])
            for side, device in ((0, right[which]), (1, left[which])):
                copy = remote(own, own, sn.at[which, d, side], rn.at[which, d, side], device)
                copy.start() if start else copy.wait_send()

    def to_far(step, start):
        for which in (0, 1):
            d = ORDER_IN[which][step]
            for side, device in ((0, right[which]), (1, left[which])):
                origin = (pos[which] + (3 if side == 0 else 1)) % 4
                if start:
                    arrived(gathered[which].at[d, rows(origin)], rn.at[which, d, side])
                part = gathered[which].at[d, rows(origin, HALF, side * HALF)]
                copy = remote(part, part, sf.at[which, d, side], rf.at[which, d, side], device)
                copy.start() if start else copy.wait_send()

    def complete(step):
        for which in (0, 1):
            d = ORDER_IN[which][step]
            for side in (0, 1):
                arrived(gathered[which].at[d, rows((pos[which] + 2) % 4, HALF, side * HALF)], rf.at[which, d, side])

    def scores(d, slot):
        part = lax.dot_general(
            pg[d, rows(slot), :], qg[d], (((1,), (1,)), ((), ())), preferred_element_type=F32
        )
        if d == 0:
            tile[rows(slot), :] = part
        else:
            tile[rows(slot), :] += part

    def all_scores(d):
        pl.loop(0, 4)(lambda slot: scores(d, slot))

    to_next(0, True)
    to_next(1, True)
    to_far(0, True)
    to_next(2, True)
    to_far(1, True)
    complete(0)
    all_scores(0)
    to_next(3, True)
    to_far(2, True)
    complete(1)
    complete(2)
    all_scores(1)
    to_far(3, True)
    all_scores(3)
    complete(3)

    def give_tile(j):
        return remote(
            tile.at[rows(2 * (1 - c) + j)], tile_in.at[pl.ds(j * BR, BR)], sst.at[j], rt.at[j], other
        )

    for j in (0, 1):
        scores(2, 2 * (1 - c) + j)
        give_tile(j).start()
    for j in (0, 1):
        scores(2, 2 * c + j)

    lane = lax.broadcasted_iota(jnp.int32, (1, TILE), 1)
    lanes = lax.broadcasted_iota(jnp.int32, (SUB, TILE), 1)
    subs = lax.broadcasted_iota(jnp.int32, (SUB, TILE), 0)
    eye = lanes - subs

    def diagonal(j):
        return jnp.where((2 * c + j == x) & (h == l), y * BR, -2 * TILE)

    def fold(op, acc, value):
        for k in range(0, SUB, 8):
            acc = op(acc, value[k:k + 8, :])
        return acc

    top = jnp.full((8, TILE), NEG, F32)
    diag = jnp.zeros((8, TILE), F32)
    for j in (0, 1):
        block = ((2 * c + j) * 4 + y) * 2 + l
        allow = None
        for yy in (3, 2, 1, 0):
            mine = (x * 4 + yy) * 2 + h
            flag = jnp.where(mine == block, 1, pairs_ref[mine, block])
            allow = jnp.full((1, TILE), flag, jnp.int32) if allow is None else jnp.where(lane < (yy + 1) * BR, flag, allow)
        allowed = jnp.broadcast_to(allow, (SUB, TILE)) == 1
        start = diagonal(j)
        arrived(tile_in.at[pl.ds(j * BR, BR)], rt.at[j])

        def first(i, carry):
            top, diag = carry
            here = rows(2 * c + j, SUB, i * SUB)
            value = (tile[here, :] + tile_in[pl.ds(pl.multiple_of(j * BR + i * SUB, SUB), SUB), :]) * SCALE
            diag = fold(jnp.add, diag, jnp.where(eye == start + i * SUB, value, 0.0))
            value = jnp.where(allowed, value, NEG)
            tile[here, :] = value
            return fold(jnp.maximum, top, value), diag

        top, diag = lax.fori_loop(0, BR // SUB, first, (top, diag))
    top = jnp.max(top, axis=0, keepdims=True)
    diag = jnp.sum(diag, axis=0, keepdims=True)

    total = jnp.zeros((8, TILE), F32)
    for j in (0, 1):

        def second(i, total):
            here = rows(2 * c + j, SUB, i * SUB)
            value = tile[here, :]
            value = jnp.where(value == NEG, 0.0, jnp.exp(value - top))
            tile[here, :] = value
            return fold(jnp.add, total, value)

        total = lax.fori_loop(0, BR // SUB, second, total)
    total = jnp.sum(total, axis=0, keepdims=True)

    sub = lax.broadcasted_iota(jnp.int32, (8, TILE), 0)
    mine = (y * 2 + l) * 2 + c
    stat[...] = jnp.where(sub == 0, top, jnp.where(sub == 1, total, diag))
    stats[mine] = stat[...]
    stat_copies = [
        remote(stat, stats.at[mine], sstat.at[i], rst.at[mine], peer) for i, peer in enumerate(stat_peers)
    ]
    for copy in stat_copies:
        copy.start()
    for slot in range(16):
        pl.when(slot != mine)(lambda slot=slot: arrived(stats.at[slot], rst.at[slot]))
    highest = stats[0, 0:1, :]
    for slot in range(1, 16):
        highest = jnp.maximum(highest, stats[slot, 0:1, :])
    totals = jnp.zeros((1, TILE), F32)
    positive = jnp.zeros((1, TILE), F32)
    for slot in range(16):
        totals = totals + stats[slot, 1:2, :] * jnp.exp(stats[slot, 0:1, :] - highest)
        positive = positive + stats[slot, 2:3, :]
    factor = jnp.exp(top - highest) / totals

    for j in (0, 1):
        start = diagonal(j)

        def third(i, _):
            here = rows(2 * c + j, SUB, i * SUB)
            value = tile[here, :] * factor - jnp.where(eye == start + i * SUB, 1.0, 0.0)
            wp[here, :] = value.astype(BF16)
            return _

        lax.fori_loop(0, BR // SUB, third, 0)
    my_rows = pl.ds(pl.multiple_of(c * CORE, CORE), CORE)
    give_wp = remote(wp.at[my_rows], wp.at[my_rows], sw.at[0], rw.at[0], other)
    give_wp.start()
    wq[c] = jnp.transpose(wp[my_rows, :])
    give_wq = remote(wq.at[c], wq.at[c], sw.at[1], rw.at[1], other)
    give_wq.start()

    group = x * 2 + h
    lossv[...] = jnp.full((8, 128), jnp.sum(highest + jnp.log(totals) - positive), F32)
    losses[group] = lossv[...]
    loss_copies = [
        remote(lossv, losses.at[group], sl.at[i], rl.at[group], peer) for i, peer in enumerate(loss_peers)
    ]
    for copy in loss_copies:
        copy.start()

    other_rows = pl.ds(pl.multiple_of((1 - c) * CORE, CORE), CORE)
    arrived(wp.at[other_rows], rw.at[0])
    arrived(wq.at[1 - c], rw.at[1])

    def gradient(which, d, slot):
        if which == 1:
            return jnp.dot(wp[rows(slot), :], qg[d], preferred_element_type=F32)
        return jnp.dot(wq[0, rows(slot), :], pg[d, 0:CORE, :], preferred_element_type=F32) + jnp.dot(
            wq[1, rows(slot), :], pg[d, CORE:TILE, :], preferred_element_type=F32
        )

    def far_copy(which, d, side):
        return remote(
            st_f.at[which, d, pl.ds(side * HALF, HALF)], in_f.at[which, d, side],
            sf5.at[which, d, side], rf5.at[which, d, side], (right, left)[side][which],
        )

    def next_copy(which, d, side):
        return remote(
            st_n.at[which, d, side], in_n.at[which, d, side],
            sn5.at[which, d, side], rn5.at[which, d, side], (right, left)[side][which],
        )

    def z_copy(which, d):
        owner = (h, l)[which]
        member = (z % 2, (z + 1) % 2)[which]
        dst = in_z.at[which, member, c]
        return owner, dst, remote(
            st_z.at[which, d], dst, sz.at[which, d], rz.at[which, member, c], dev(x, y, owner, (z + d) % 4)
        )

    def send_far(step):
        for which in (0, 1):
            d = ORDER_OUT[which][step]
            st_f[which, d] = gradient(which, d, (pos[which] + 2) % 4).astype(BF16)
            for side in (0, 1):
                far_copy(which, d, side).start()

    def send_next(step):
        for which in (0, 1):
            d = ORDER_OUT[which][step]
            for side in (0, 1):
                part = gradient(which, d, (pos[which] + (1, 3)[side]) % 4)
                add, keep = slice(side * HALF, (side + 1) * HALF), slice((1 - side) * HALF, (2 - side) * HALF)
                st_n[which, d, side, keep] = part[keep].astype(BF16)
                arrived(in_f.at[which, d, side], rf5.at[which, d, side])
                st_n[which, d, side, add] = (part[add] + in_f[which, d, side].astype(F32)).astype(BF16)
                next_copy(which, d, side).start()

    def send_home(step):
        for which in (0, 1):
            d = ORDER_OUT[which][step]
            part = gradient(which, d, pos[which])
            for side in (0, 1):
                arrived(in_n.at[which, d, side], rn5.at[which, d, side])
                part = part + in_n[which, d, side].astype(F32)
            st_z[which, d] = part.astype(BF16)
            owner, dst, copy = z_copy(which, d)
            if d == 0:
                member = (z % 2, (z + 1) % 2)[which]

                @pl.when(owner == c)
                def _():
                    pltpu.make_async_copy(st_z.at[which, d], dst, rz.at[which, member, c]).start()

                @pl.when(owner != c)
                def _():
                    copy.start()
            else:
                copy.start()

    send_far(0)
    send_far(1)
    send_next(0)
    send_far(2)
    send_next(1)
    send_home(0)
    send_far(3)
    send_next(2)
    send_home(1)
    send_next(3)
    send_home(2)
    send_home(3)

    along_z(False)
    for step in range(4):
        to_next(step, False)
        to_far(step, False)
    for j in (0, 1):
        give_tile(j).wait_send()
    for copy in stat_copies:
        copy.wait_send()
    give_wp.wait_send()
    give_wq.wait_send()
    for copy in loss_copies:
        copy.wait_send()
    for which in (0, 1):
        for d in range(4):
            for side in (0, 1):
                far_copy(which, d, side).wait_send()
                next_copy(which, d, side).wait_send()

    for slot in range(8):
        pl.when(slot != group)(lambda slot=slot: arrived(losses.at[slot], rl.at[slot]))
    loss = losses[0]
    for slot in range(1, 8):
        loss = loss + losses[slot]
    loss_ref[0, 0] = loss[0, 0] / (32 * BR)

    for which, out in ((0, gq_ref), (1, gp_ref)):
        for part in (0, 1):
            for member in (0, 1):
                arrived(in_z.at[which, member, part], rz.at[which, member, part])
            out[:, part * WC:(part + 1) * WC] = (
                in_z[which, 0, part].astype(F32) + in_z[which, 1, part].astype(F32)
            ).astype(BF16)
    for which in (0, 1):
        for d in range(4):
            owner, _, copy = z_copy(which, d)
            if d == 0:
                pl.when(owner != c)(lambda copy=copy: copy.wait_send())
            else:
                copy.wait_send()


def body(queries, passages, pairs):
    dma = pltpu.SemaphoreType.DMA
    loss, grad_queries, grad_passages = pl.pallas_call(
        kernel,
        out_shape=(
            jax.ShapeDtypeStruct((1, 1), F32),
            jax.ShapeDtypeStruct(queries.shape, BF16),
            jax.ShapeDtypeStruct(passages.shape, BF16),
        ),
        in_specs=[
            pl.BlockSpec(memory_space=pl.ANY),
            pl.BlockSpec(memory_space=pl.ANY),
            pl.BlockSpec(memory_space=pltpu.SMEM),
        ],
        out_specs=(
            pl.BlockSpec(memory_space=pltpu.SMEM),
            pl.BlockSpec(memory_space=pltpu.VMEM),
            pl.BlockSpec(memory_space=pltpu.VMEM),
        ),
        scratch_shapes=[
            pltpu.VMEM((4, TILE, WC), BF16),
            pltpu.VMEM((4, TILE, WC), BF16),
            pltpu.VMEM((TILE, TILE), F32),
            pltpu.VMEM((CORE, TILE), F32),
            pltpu.VMEM((TILE, TILE), BF16),
            pltpu.VMEM((2, TILE, CORE), BF16),
            pltpu.VMEM((2, 4, BR, WC), BF16),
            pltpu.VMEM((2, 4, 2, HALF, WC), BF16),
            pltpu.VMEM((2, 4, 2, BR, WC), BF16),
            pltpu.VMEM((2, 4, 2, BR, WC), BF16),
            pltpu.VMEM((2, 4, BR, WC), BF16),
            pltpu.VMEM((2, 2, 2, BR, WC), BF16),
            pltpu.VMEM((8, TILE), F32),
            pltpu.VMEM((16, 8, TILE), F32),
            pltpu.VMEM((8, 128), F32),
            pltpu.VMEM((8, 8, 128), F32),
            dma((2, 4)), dma((2, 4, 2)),
            dma((2, 4, 2)), dma((2, 4, 2)),
            dma((2, 4, 2)), dma((2, 4, 2)),
            dma((2,)), dma((2,)),
            dma((16,)), dma((15,)),
            dma((2,)), dma((2,)),
            dma((2, 4, 2)), dma((2, 4, 2)),
            dma((2, 4, 2)), dma((2, 4, 2)),
            dma((2, 2, 2)), dma((2, 4)),
            dma((8,)), dma((7,)),
        ],
        compiler_params=pltpu.CompilerParams(
            collective_id=0, has_side_effects=True, vmem_limit_bytes=56 * 2**20
        ),
    )(queries, passages, pairs)
    return loss.reshape(()), grad_queries, grad_passages


def solution(mesh):
    return jax.shard_map(
        body,
        mesh=mesh,
        in_specs=(P("blk", "wid"), P("blk", "wid"), P()),
        out_specs=(P(), P("blk", "wid"), P("blk", "wid")),
        check_vma=False,
    )
```

```python
import jax
import jax.numpy as jnp
from jax import lax
from jax.experimental import pallas as pl
from jax.experimental.pallas import tpu as pltpu
from jax.sharding import PartitionSpec as P

MESH = pl.DeviceIdType.MESH
BR = 224
HALF = BR // 2
WC = 512
TILE = 4 * BR
CORE = 2 * BR
SUB = 32
NEG = -1e30
SCALE = 4096 ** -0.5
ORDER_IN = ((0, 1, 3, 2), (0, 3, 1, 2))
ORDER_OUT = ((2, 1, 3, 0), (2, 3, 1, 0))
F32 = jnp.float32
BF16 = jnp.bfloat16


def rows(slot, n=BR, off=0):
    return pl.ds(pl.multiple_of(slot * BR + off, 16), n)


def kernel(
    q_hbm, p_hbm, pairs_ref, loss_ref, in_q, in_p,
    qg, pg, tile, tile_in, wp, wq, st_f, in_f, st_n, in_n, st_z, stat, stats, lossv, losses,
    r1, s1, rn, sn, rf, sf, rt, sst, rst, sstat, rw, sw, rf5, sf5, rn5, sn5, rz, sz, rl, sl,
):
    blk = lax.axis_index("blk")
    z = lax.axis_index("wid")
    x = blk // 8
    y = (blk // 2) % 4
    c = blk % 2
    h = z // 2
    l = ((z + 1) // 2) % 2
    twin = h * 2 + (z + 1) % 2
    flip = 3 - z
    far_x, far_y = (x + 2) % 4, (y + 2) % 4

    def dev(xx, yy, cc, zz):
        return ((xx * 4 + yy) * 2 + cc, zz)

    right = (dev(x, (y + 1) % 4, c, z), dev((x + 1) % 4, y, c, z))
    left = (dev(x, (y + 3) % 4, c, z), dev((x + 3) % 4, y, c, z))
    other = dev(x, y, 1 - c, z)
    gathered = (qg, pg)
    pos = (y, x)

    def remote(src, dst, ssem, rsem, device):
        return pltpu.make_async_remote_copy(
            src_ref=src, dst_ref=dst, send_sem=ssem, recv_sem=rsem, device_id=device, device_id_type=MESH
        )

    def arrived(dst, sem):
        pltpu.make_async_copy(dst, dst, sem).wait()

    barrier = pltpu.get_barrier_semaphore()
    peers = [other]
    for dz in (1, 2, 3):
        for cc in (0, 1):
            peers.append(dev(x, y, cc, (z + dz) % 4))
    stat_peers = [other, dev(x, y, c, twin), dev(x, y, 1 - c, twin)]
    for dy in (1, 2, 3):
        for cc in (0, 1):
            for zz in (z, twin):
                peers.append(dev(x, (y + dy) % 4, cc, zz))
                stat_peers.append(peers[-1])
    loss_peers = [dev(x, y, c, flip)]
    for dx in (1, 2, 3):
        for zz in (z, flip):
            peers.append(dev((x + dx) % 4, y, c, zz))
            loss_peers.append(peers[-1])
    for peer in peers:
        pl.semaphore_signal(barrier, inc=1, device_id=peer, device_id_type=MESH)
    pl.semaphore_wait(barrier, len(peers))

    def along_z(step, start):
        for which in (0, 1):
            d = ORDER_IN[which][step]
            zt = (z + 4 - d) % 4
            owner = zt // 2 if which == 0 else ((zt + 1) // 2) % 2

            @pl.when(owner == c)
            def _():
                for part in (0, 1):
                    src = (q_hbm, p_hbm)[which].at[:, part * WC:(part + 1) * WC]
                    dst = gathered[which].at[d, rows(pos[which])]
                    copy = remote(src, dst, s1.at[which, d, part], r1.at[which, d], dev(x, y, part, zt))
                    if d == 0:
                        if start:
                            @pl.when(c == part)
                            def _():
                                pltpu.make_async_copy(src, dst, r1.at[which, d]).start()

                        @pl.when(c != part)
                        def _():
                            copy.start() if start else copy.wait_send()
                    else:
                        copy.start() if start else copy.wait_send()

    along_z(0, True)
    along_z(1, True)

    def to_next(step, start):
        for which in (0, 1):
            d = ORDER_IN[which][step]
            own = gathered[which].at[d, rows(pos[which])]
            if start:
                arrived(own, r1.at[which, d])
            for side, device in ((0, right[which]), (1, left[which])):
                copy = remote(own, own, sn.at[which, d, side], rn.at[which, d, side], device)
                copy.start() if start else copy.wait_send()

    def to_far(step, start):
        for which in (0, 1):
            d = ORDER_IN[which][step]
            for side, device in ((0, right[which]), (1, left[which])):
                origin = (pos[which] + (3 if side == 0 else 1)) % 4
                if start:
                    arrived(gathered[which].at[d, rows(origin)], rn.at[which, d, side])
                part = gathered[which].at[d, rows(origin, HALF, side * HALF)]
                copy = remote(part, part, sf.at[which, d, side], rf.at[which, d, side], device)
                copy.start() if start else copy.wait_send()

    def complete(step):
        for which in (0, 1):
            d = ORDER_IN[which][step]
            for side in (0, 1):
                arrived(gathered[which].at[d, rows((pos[which] + 2) % 4, HALF, side * HALF)], rf.at[which, d, side])

    def scores(d, slot):
        part = lax.dot_general(
            pg[d, rows(slot), :], qg[d], (((1,), (1,)), ((), ())), preferred_element_type=F32
        )
        if d == 0:
            tile[rows(slot), :] = part
        else:
            tile[rows(slot), :] += part

    def all_scores(d):
        pl.loop(0, 4)(lambda slot: scores(d, slot))

    to_next(0, True)
    to_next(1, True)
    along_z(1, False)
    along_z(2, True)
    to_far(0, True)
    to_next(2, True)
    along_z(2, False)
    along_z(3, True)
    to_far(1, True)
    complete(0)
    all_scores(0)
    to_far(2, True)
    to_next(3, True)
    complete(1)
    complete(2)
    all_scores(1)
    to_far(3, True)
    all_scores(3)
    complete(3)

    def give_tile(j):
        return remote(
            tile.at[rows(2 * (1 - c) + j)], tile_in.at[pl.ds(j * BR, BR)], sst.at[j], rt.at[j], other
        )

    for j in (0, 1):
        scores(2, 2 * (1 - c) + j)
        give_tile(j).start()
    for j in (0, 1):
        scores(2, 2 * c + j)

    lane = lax.broadcasted_iota(jnp.int32, (1, TILE), 1)
    lanes = lax.broadcasted_iota(jnp.int32, (SUB, TILE), 1)
    subs = lax.broadcasted_iota(jnp.int32, (SUB, TILE), 0)
    eye = lanes - subs

    def diagonal(j):
        return jnp.where((2 * c + j == x) & (h == l), y * BR, -2 * TILE)

    def fold(op, acc, value):
        for k in range(0, SUB, 8):
            acc = op(acc, value[k:k + 8, :])
        return acc

    top = jnp.full((8, TILE), NEG, F32)
    diag = jnp.zeros((8, TILE), F32)
    for j in (0, 1):
        block = ((2 * c + j) * 4 + y) * 2 + l
        allow = None
        for yy in (3, 2, 1, 0):
            mine = (x * 4 + yy) * 2 + h
            flag = jnp.where(mine == block, 1, pairs_ref[mine, block])
            allow = jnp.full((1, TILE), flag, jnp.int32) if allow is None else jnp.where(lane < (yy + 1) * BR, flag, allow)
        allowed = jnp.broadcast_to(allow, (SUB, TILE)) == 1
        start = diagonal(j)
        arrived(tile_in.at[pl.ds(j * BR, BR)], rt.at[j])

        def first(i, carry):
            top, diag = carry
            here = rows(2 * c + j, SUB, i * SUB)
            value = (tile[here, :] + tile_in[pl.ds(pl.multiple_of(j * BR + i * SUB, SUB), SUB), :]) * SCALE
            diag = fold(jnp.add, diag, jnp.where(eye == start + i * SUB, value, 0.0))
            value = jnp.where(allowed, value, NEG)
            tile[here, :] = value
            return fold(jnp.maximum, top, value), diag

        top, diag = lax.fori_loop(0, BR // SUB, first, (top, diag))
    top = jnp.max(top, axis=0, keepdims=True)
    diag = jnp.sum(diag, axis=0, keepdims=True)

    total = jnp.zeros((8, TILE), F32)
    for j in (0, 1):

        def second(i, total):
            here = rows(2 * c + j, SUB, i * SUB)
            value = tile[here, :]
            value = jnp.where(value == NEG, 0.0, jnp.exp(value - top))
            tile[here, :] = value
            return fold(jnp.add, total, value)

        total = lax.fori_loop(0, BR // SUB, second, total)
    total = jnp.sum(total, axis=0, keepdims=True)

    def pack(row):
        parts = [row[:, k * 128:(k + 1) * 128] for k in range(TILE // 128)]
        return jnp.concatenate(parts + [jnp.zeros((1, 128), F32)], axis=0)

    def unpack(block):
        return jnp.concatenate([block[k:k + 1, :] for k in range(TILE // 128)], axis=1)

    mine = (y * 2 + l) * 2 + c
    stat[0:8, :] = pack(jnp.where(total > 0, top + jnp.log(total), NEG))
    stat[8:16, :] = pack(diag)
    stats[mine] = stat[...]
    stat_copies = [
        remote(stat, stats.at[mine], sstat.at[i], rst.at[mine], peer) for i, peer in enumerate(stat_peers)
    ]
    for copy in stat_copies:
        copy.start()
    for slot in range(16):
        pl.when(slot != mine)(lambda slot=slot: arrived(stats.at[slot], rst.at[slot]))
    highest = stats[0, 0:8, :]
    for slot in range(1, 16):
        highest = jnp.maximum(highest, stats[slot, 0:8, :])
    totals = jnp.zeros((8, 128), F32)
    positive = jnp.zeros((8, 128), F32)
    for slot in range(16):
        totals = totals + jnp.exp(stats[slot, 0:8, :] - highest)
        positive = positive + stats[slot, 8:16, :]
    log_total = highest + jnp.log(totals)
    factor = jnp.exp(top - unpack(log_total))

    for j in (0, 1):
        start = diagonal(j)

        def third(i, _):
            here = rows(2 * c + j, SUB, i * SUB)
            value = tile[here, :] * factor - jnp.where(eye == start + i * SUB, 1.0, 0.0)
            wp[here, :] = value.astype(BF16)
            return _

        lax.fori_loop(0, BR // SUB, third, 0)
    my_rows = pl.ds(pl.multiple_of(c * CORE, CORE), CORE)
    give_wp = remote(wp.at[my_rows], wp.at[my_rows], sw.at[0], rw.at[0], other)
    give_wp.start()
    wq[c] = jnp.transpose(wp[my_rows, :])
    give_wq = remote(wq.at[c], wq.at[c], sw.at[1], rw.at[1], other)
    give_wq.start()

    group = x * 2 + h
    row = lax.broadcasted_iota(jnp.int32, (8, 128), 0)
    lossv[...] = jnp.full((8, 128), jnp.sum(jnp.where(row < TILE // 128, log_total - positive, 0.0)), F32)
    losses[group] = lossv[...]
    loss_copies = [
        remote(lossv, losses.at[group], sl.at[i], rl.at[group], peer) for i, peer in enumerate(loss_peers)
    ]
    for copy in loss_copies:
        copy.start()

    other_rows = pl.ds(pl.multiple_of((1 - c) * CORE, CORE), CORE)
    arrived(wp.at[other_rows], rw.at[0])

    def gradient(which, d, slot):
        if which == 1:
            return jnp.dot(wp[rows(slot), :], qg[d], preferred_element_type=F32)
        return jnp.dot(wq[0, rows(slot), :], pg[d, 0:CORE, :], preferred_element_type=F32) + jnp.dot(
            wq[1, rows(slot), :], pg[d, CORE:TILE, :], preferred_element_type=F32
        )

    def far_copy(which, d, side):
        return remote(
            st_f.at[which, d, pl.ds(side * HALF, HALF)], in_f.at[which, d, side],
            sf5.at[which, d, side], rf5.at[which, d, side], (right, left)[side][which],
        )

    def next_copy(which, d, side):
        return remote(
            st_n.at[which, d, side], in_n.at[which, d, side],
            sn5.at[which, d, side], rn5.at[which, d, side], (right, left)[side][which],
        )

    def z_copy(which, d):
        owner = (h, l)[which]
        member = (z % 2, (z + 1) % 2)[which]
        dst = (in_q, in_p)[which].at[member, :, pl.ds(pl.multiple_of(c * WC, WC), WC)]
        return owner, dst, remote(
            st_z.at[which, d], dst, sz.at[which, d], rz.at[which, member, c], dev(x, y, owner, (z + d) % 4)
        )

    def send_far(step):
        for which in (1, 0):
            d = ORDER_OUT[which][step]
            if which == 0 and step == 0:
                arrived(wq.at[1 - c], rw.at[1])
            st_f[which, d] = gradient(which, d, (pos[which] + 2) % 4).astype(BF16)
            for side in (0, 1):
                far_copy(which, d, side).start()

    def send_next(step):
        for which in (1, 0):
            d = ORDER_OUT[which][step]
            for side in (0, 1):
                part = gradient(which, d, (pos[which] + (1, 3)[side]) % 4)
                add, keep = slice(side * HALF, (side + 1) * HALF), slice((1 - side) * HALF, (2 - side) * HALF)
                st_n[which, d, side, keep] = part[keep].astype(BF16)
                arrived(in_f.at[which, d, side], rf5.at[which, d, side])
                st_n[which, d, side, add] = (part[add] + in_f[which, d, side].astype(F32)).astype(BF16)
                next_copy(which, d, side).start()

    def send_home(step):
        for which in (1, 0):
            d = ORDER_OUT[which][step]
            part = gradient(which, d, pos[which])
            for side in (0, 1):
                arrived(in_n.at[which, d, side], rn5.at[which, d, side])
                part = part + in_n[which, d, side].astype(F32)
            st_z[which, d] = part.astype(BF16)
            owner, dst, copy = z_copy(which, d)
            if d == 0:
                member = (z % 2, (z + 1) % 2)[which]

                @pl.when(owner == c)
                def _():
                    pltpu.make_async_copy(st_z.at[which, d], dst, rz.at[which, member, c]).start()

                @pl.when(owner != c)
                def _():
                    copy.start()
            else:
                copy.start()

    send_far(0)
    send_far(1)
    send_next(0)
    send_far(2)
    send_next(1)
    send_home(0)
    send_far(3)
    send_next(2)
    send_home(1)
    send_next(3)
    send_home(2)
    send_home(3)

    along_z(0, False)
    along_z(3, False)
    for step in range(4):
        to_next(step, False)
        to_far(step, False)
    for j in (0, 1):
        give_tile(j).wait_send()
    for copy in stat_copies:
        copy.wait_send()
    give_wp.wait_send()
    give_wq.wait_send()
    for copy in loss_copies:
        copy.wait_send()
    for which in (0, 1):
        for d in range(4):
            for side in (0, 1):
                far_copy(which, d, side).wait_send()
                next_copy(which, d, side).wait_send()

    for slot in range(8):
        pl.when(slot != group)(lambda slot=slot: arrived(losses.at[slot], rl.at[slot]))
    loss = losses[0]
    for slot in range(1, 8):
        loss = loss + losses[slot]
    loss_ref[0, 0] = loss[0, 0] / (32 * BR)

    for which in (0, 1):
        for part in (0, 1):
            for member in (0, 1):
                arrived((in_q, in_p)[which].at[member, :, part * WC:(part + 1) * WC], rz.at[which, member, part])
    for which in (0, 1):
        for d in range(4):
            owner, _, copy = z_copy(which, d)
            if d == 0:
                pl.when(owner != c)(lambda copy=copy: copy.wait_send())
            else:
                copy.wait_send()


def body(queries, passages, pairs):
    dma = pltpu.SemaphoreType.DMA
    loss, in_q, in_p = pl.pallas_call(
        kernel,
        out_shape=(
            jax.ShapeDtypeStruct((1, 1), F32),
            jax.ShapeDtypeStruct((2, *queries.shape), BF16),
            jax.ShapeDtypeStruct((2, *passages.shape), BF16),
        ),
        in_specs=[
            pl.BlockSpec(memory_space=pl.ANY),
            pl.BlockSpec(memory_space=pl.ANY),
            pl.BlockSpec(memory_space=pltpu.SMEM),
        ],
        out_specs=(
            pl.BlockSpec(memory_space=pltpu.SMEM),
            pl.BlockSpec(memory_space=pl.ANY),
            pl.BlockSpec(memory_space=pl.ANY),
        ),
        scratch_shapes=[
            pltpu.VMEM((4, TILE, WC), BF16),
            pltpu.VMEM((4, TILE, WC), BF16),
            pltpu.VMEM((TILE, TILE), F32),
            pltpu.VMEM((CORE, TILE), F32),
            pltpu.VMEM((TILE, TILE), BF16),
            pltpu.VMEM((2, TILE, CORE), BF16),
            pltpu.VMEM((2, 4, BR, WC), BF16),
            pltpu.VMEM((2, 4, 2, HALF, WC), BF16),
            pltpu.VMEM((2, 4, 2, BR, WC), BF16),
            pltpu.VMEM((2, 4, 2, BR, WC), BF16),
            pltpu.VMEM((2, 4, BR, WC), BF16),
            pltpu.VMEM((16, 128), F32),
            pltpu.VMEM((16, 16, 128), F32),
            pltpu.VMEM((8, 128), F32),
            pltpu.VMEM((8, 8, 128), F32),
            dma((2, 4)), dma((2, 4, 2)),
            dma((2, 4, 2)), dma((2, 4, 2)),
            dma((2, 4, 2)), dma((2, 4, 2)),
            dma((2,)), dma((2,)),
            dma((16,)), dma((15,)),
            dma((2,)), dma((2,)),
            dma((2, 4, 2)), dma((2, 4, 2)),
            dma((2, 4, 2)), dma((2, 4, 2)),
            dma((2, 2, 2)), dma((2, 4)),
            dma((8,)), dma((7,)),
        ],
        compiler_params=pltpu.CompilerParams(
            collective_id=0, has_side_effects=True, vmem_limit_bytes=56 * 2**20
        ),
    )(queries, passages, pairs)
    grads = [(pair[0].astype(F32) + pair[1].astype(F32)).astype(BF16) for pair in (in_q, in_p)]
    return loss.reshape(()), *grads


def solution(mesh):
    return jax.shard_map(
        body,
        mesh=mesh,
        in_specs=(P("blk", "wid"), P("blk", "wid"), P()),
        out_specs=(P(), P("blk", "wid"), P("blk", "wid")),
        check_vma=False,
    )
```

```python
import jax
import jax.numpy as jnp
from jax import lax
from jax.experimental import pallas as pl
from jax.experimental.pallas import tpu as pltpu
from jax.sharding import PartitionSpec as P

MESH = pl.DeviceIdType.MESH
BR = 224
HALF = BR // 2
WC = 512
TILE = 4 * BR
CORE = 2 * BR
SUB = 32
NEG = -1e30
SCALE = 4096 ** -0.5
ORDER_IN = ((0, 1, 3, 2), (0, 3, 1, 2))
ORDER_OUT = ((2, 1, 3, 0), (2, 3, 1, 0))
F32 = jnp.float32
BF16 = jnp.bfloat16


def rows(slot, n=BR, off=0):
    return pl.ds(pl.multiple_of(slot * BR + off, 16), n)


def kernel(
    q_hbm, p_hbm, pairs_ref, loss_ref, in_q, in_p,
    qg, pg, tile, tile_in, wp, wq, st_f, in_f, st_n, in_n, st_z, stat, stats, lossv, losses,
    r1, s1, s0, rn, sn, rf, sf, rt, sst, rst, sstat, rw, sw, rf5, sf5, rn5, sn5, rz, sz, rl, sl,
):
    blk = lax.axis_index("blk")
    z = lax.axis_index("wid")
    x = blk // 8
    y = (blk // 2) % 4
    c = blk % 2
    h = z // 2
    l = ((z + 1) // 2) % 2
    twin = h * 2 + (z + 1) % 2
    flip = 3 - z
    far_x, far_y = (x + 2) % 4, (y + 2) % 4

    def dev(xx, yy, cc, zz):
        return ((xx * 4 + yy) * 2 + cc, zz)

    right = (dev(x, (y + 1) % 4, c, z), dev((x + 1) % 4, y, c, z))
    left = (dev(x, (y + 3) % 4, c, z), dev((x + 3) % 4, y, c, z))
    other = dev(x, y, 1 - c, z)
    gathered = (qg, pg)
    pos = (y, x)

    def remote(src, dst, ssem, rsem, device):
        return pltpu.make_async_remote_copy(
            src_ref=src, dst_ref=dst, send_sem=ssem, recv_sem=rsem, device_id=device, device_id_type=MESH
        )

    def arrived(dst, sem):
        pltpu.make_async_copy(dst, dst, sem).wait()

    barrier = pltpu.get_barrier_semaphore()
    peers = [other]
    for device in (*right, *left):
        peers.append(device)
        peers.append((device[0] + 1 - 2 * c, device[1]))
    for dz in (1, 2, 3):
        for cc in (0, 1):
            peers.append(dev(x, y, cc, (z + dz) % 4))
    for peer in peers:
        pl.semaphore_signal(barrier, inc=1, device_id=peer, device_id_type=MESH)
    pl.semaphore_wait(barrier, len(peers))
    stat_peers = [other, dev(x, y, c, twin), dev(x, y, 1 - c, twin)]
    for dy in (1, 2, 3):
        for cc in (0, 1):
            for zz in (z, twin):
                stat_peers.append(dev(x, (y + dy) % 4, cc, zz))
    loss_peers = [dev(x, y, c, flip)]
    for dx in (1, 2, 3):
        for zz in (z, flip):
            loss_peers.append(dev((x + dx) % 4, y, c, zz))

    def along_z(step, start):
        for which in (0, 1):
            d = ORDER_IN[which][step]
            zt = (z + 4 - d) % 4
            owner = zt // 2 if which == 0 else ((zt + 1) // 2) % 2

            @pl.when(owner == c)
            def _():
                for part in (0, 1):
                    src = (q_hbm, p_hbm)[which].at[:, part * WC:(part + 1) * WC]
                    dst = gathered[which].at[d, rows(pos[which])]
                    copy = remote(src, dst, s1.at[which, d, part], r1.at[which, d], dev(x, y, part, zt))
                    if d == 0:
                        for side, device in ((0, right[which]), (1, left[which])):
                            direct = remote(
                                src, dst, s0.at[which, part, side], rn.at[which, d, side],
                                (device[0] - c + part, device[1]),
                            )
                            direct.start() if start else direct.wait_send()
                        if start:
                            @pl.when(c == part)
                            def _():
                                pltpu.make_async_copy(src, dst, r1.at[which, d]).start()

                        @pl.when(c != part)
                        def _():
                            copy.start() if start else copy.wait_send()
                    else:
                        copy.start() if start else copy.wait_send()

    along_z(0, True)
    along_z(1, True)

    def to_next(step, start):
        for which in (0, 1):
            d = ORDER_IN[which][step]
            own = gathered[which].at[d, rows(pos[which])]
            if start:
                arrived(own, r1.at[which, d])
            for side, device in ((0, right[which]), (1, left[which])):
                copy = remote(own, own, sn.at[which, d, side], rn.at[which, d, side], device)
                copy.start() if start else copy.wait_send()

    def to_far(step, start):
        for which in (0, 1):
            d = ORDER_IN[which][step]
            for side, device in ((0, right[which]), (1, left[which])):
                origin = (pos[which] + (3 if side == 0 else 1)) % 4
                if start:
                    arrived(gathered[which].at[d, rows(origin)], rn.at[which, d, side])
                part = gathered[which].at[d, rows(origin, HALF, side * HALF)]
                copy = remote(part, part, sf.at[which, d, side], rf.at[which, d, side], device)
                copy.start() if start else copy.wait_send()

    def complete(step):
        for which in (0, 1):
            d = ORDER_IN[which][step]
            for side in (0, 1):
                arrived(gathered[which].at[d, rows((pos[which] + 2) % 4, HALF, side * HALF)], rf.at[which, d, side])

    def scores(d, slot):
        part = lax.dot_general(
            pg[d, rows(slot), :], qg[d], (((1,), (1,)), ((), ())), preferred_element_type=F32
        )
        if d == 0:
            tile[rows(slot), :] = part
        else:
            tile[rows(slot), :] += part

    def all_scores(d):
        pl.loop(0, 4)(lambda slot: scores(d, slot))

    to_next(1, True)
    along_z(1, False)
    along_z(2, True)
    to_far(0, True)
    to_next(2, True)
    along_z(2, False)
    along_z(3, True)
    to_far(1, True)
    for which in (0, 1):
        arrived(gathered[which].at[0, rows(pos[which])], r1.at[which, 0])
    complete(0)
    all_scores(0)
    to_far(2, True)
    to_next(3, True)
    complete(1)
    complete(2)
    all_scores(1)
    to_far(3, True)
    all_scores(3)
    complete(3)

    def give_tile(j):
        return remote(
            tile.at[rows(2 * (1 - c) + j)], tile_in.at[pl.ds(j * BR, BR)], sst.at[j], rt.at[j], other
        )

    for j in (0, 1):
        scores(2, 2 * (1 - c) + j)
        give_tile(j).start()
    for j in (0, 1):
        scores(2, 2 * c + j)

    lane = lax.broadcasted_iota(jnp.int32, (1, TILE), 1)
    lanes = lax.broadcasted_iota(jnp.int32, (SUB, TILE), 1)
    subs = lax.broadcasted_iota(jnp.int32, (SUB, TILE), 0)
    eye = lanes - subs

    def diagonal(j):
        return jnp.where((2 * c + j == x) & (h == l), y * BR, -2 * TILE)

    def fold(op, acc, value):
        for k in range(0, SUB, 8):
            acc = op(acc, value[k:k + 8, :])
        return acc

    top = jnp.full((8, TILE), NEG, F32)
    diag = jnp.zeros((8, TILE), F32)
    for j in (0, 1):
        block = ((2 * c + j) * 4 + y) * 2 + l
        allow = None
        for yy in (3, 2, 1, 0):
            mine = (x * 4 + yy) * 2 + h
            flag = jnp.where(mine == block, 1, pairs_ref[mine, block])
            allow = jnp.full((1, TILE), flag, jnp.int32) if allow is None else jnp.where(lane < (yy + 1) * BR, flag, allow)
        allowed = jnp.broadcast_to(allow, (SUB, TILE)) == 1
        start = diagonal(j)
        arrived(tile_in.at[pl.ds(j * BR, BR)], rt.at[j])

        def first(i, carry):
            top, diag = carry
            here = rows(2 * c + j, SUB, i * SUB)
            value = (tile[here, :] + tile_in[pl.ds(pl.multiple_of(j * BR + i * SUB, SUB), SUB), :]) * SCALE
            diag = fold(jnp.add, diag, jnp.where(eye == start + i * SUB, value, 0.0))
            value = jnp.where(allowed, value, NEG)
            tile[here, :] = value
            return fold(jnp.maximum, top, value), diag

        top, diag = lax.fori_loop(0, BR // SUB, first, (top, diag))
    top = jnp.max(top, axis=0, keepdims=True)
    diag = jnp.sum(diag, axis=0, keepdims=True)

    total = jnp.zeros((8, TILE), F32)
    for j in (0, 1):

        def second(i, total):
            here = rows(2 * c + j, SUB, i * SUB)
            value = tile[here, :]
            value = jnp.where(value == NEG, 0.0, jnp.exp(value - top))
            tile[here, :] = value
            return fold(jnp.add, total, value)

        total = lax.fori_loop(0, BR // SUB, second, total)
    total = jnp.sum(total, axis=0, keepdims=True)

    def pack(row):
        parts = [row[:, k * 128:(k + 1) * 128] for k in range(TILE // 128)]
        return jnp.concatenate(parts + [jnp.zeros((1, 128), F32)], axis=0)

    def unpack(block):
        return jnp.concatenate([block[k:k + 1, :] for k in range(TILE // 128)], axis=1)

    mine = (y * 2 + l) * 2 + c
    stat[0:8, :] = pack(jnp.where(total > 0, top + jnp.log(total), NEG))
    stat[8:16, :] = pack(diag)
    stats[mine] = stat[...]
    stat_copies = [
        remote(stat, stats.at[mine], sstat.at[i], rst.at[mine], peer) for i, peer in enumerate(stat_peers)
    ]
    for copy in stat_copies:
        copy.start()
    for slot in range(16):
        pl.when(slot != mine)(lambda slot=slot: arrived(stats.at[slot], rst.at[slot]))
    highest = stats[0, 0:8, :]
    for slot in range(1, 16):
        highest = jnp.maximum(highest, stats[slot, 0:8, :])
    totals = jnp.zeros((8, 128), F32)
    positive = jnp.zeros((8, 128), F32)
    for slot in range(16):
        totals = totals + jnp.exp(stats[slot, 0:8, :] - highest)
        positive = positive + stats[slot, 8:16, :]
    log_total = highest + jnp.log(totals)
    factor = jnp.exp(top - unpack(log_total))

    for j in (0, 1):
        start = diagonal(j)

        def third(i, _):
            here = rows(2 * c + j, SUB, i * SUB)
            value = tile[here, :] * factor - jnp.where(eye == start + i * SUB, 1.0, 0.0)
            wp[here, :] = value.astype(BF16)
            return _

        lax.fori_loop(0, BR // SUB, third, 0)
    my_rows = pl.ds(pl.multiple_of(c * CORE, CORE), CORE)
    give_wp = remote(wp.at[my_rows], wp.at[my_rows], sw.at[0], rw.at[0], other)
    give_wp.start()
    wq[c] = jnp.transpose(wp[my_rows, :])
    give_wq = remote(wq.at[c], wq.at[c], sw.at[1], rw.at[1], other)
    give_wq.start()

    group = x * 2 + h
    row = lax.broadcasted_iota(jnp.int32, (8, 128), 0)
    lossv[...] = jnp.full((8, 128), jnp.sum(jnp.where(row < TILE // 128, log_total - positive, 0.0)), F32)
    losses[group] = lossv[...]
    loss_copies = [
        remote(lossv, losses.at[group], sl.at[i], rl.at[group], peer) for i, peer in enumerate(loss_peers)
    ]
    for copy in loss_copies:
        copy.start()

    other_rows = pl.ds(pl.multiple_of((1 - c) * CORE, CORE), CORE)
    arrived(wp.at[other_rows], rw.at[0])

    def gradient(which, d, slot):
        if which == 1:
            return jnp.dot(wp[rows(slot), :], qg[d], preferred_element_type=F32)
        return jnp.dot(wq[0, rows(slot), :], pg[d, 0:CORE, :], preferred_element_type=F32) + jnp.dot(
            wq[1, rows(slot), :], pg[d, CORE:TILE, :], preferred_element_type=F32
        )

    def far_copy(which, d, side):
        return remote(
            st_f.at[which, d, pl.ds(side * HALF, HALF)], in_f.at[which, d, side],
            sf5.at[which, d, side], rf5.at[which, d, side], (right, left)[side][which],
        )

    def next_copy(which, d, side):
        return remote(
            st_n.at[which, d, side], in_n.at[which, d, side],
            sn5.at[which, d, side], rn5.at[which, d, side], (right, left)[side][which],
        )

    def z_copy(which, d):
        owner = (h, l)[which]
        member = (z % 2, (z + 1) % 2)[which]
        dst = (in_q, in_p)[which].at[member, :, pl.ds(pl.multiple_of(c * WC, WC), WC)]
        return owner, dst, remote(
            st_z.at[which, d], dst, sz.at[which, d], rz.at[which, member, c], dev(x, y, owner, (z + d) % 4)
        )

    def send_far(step):
        for which in (1, 0):
            d = ORDER_OUT[which][step]
            if which == 0 and step == 0:
                arrived(wq.at[1 - c], rw.at[1])
            st_f[which, d] = gradient(which, d, (pos[which] + 2) % 4).astype(BF16)
            for side in (0, 1):
                far_copy(which, d, side).start()

    def send_next(step):
        for which in (1, 0):
            d = ORDER_OUT[which][step]
            for side in (0, 1):
                part = gradient(which, d, (pos[which] + (1, 3)[side]) % 4)
                add, keep = slice(side * HALF, (side + 1) * HALF), slice((1 - side) * HALF, (2 - side) * HALF)
                st_n[which, d, side, keep] = part[keep].astype(BF16)
                arrived(in_f.at[which, d, side], rf5.at[which, d, side])
                st_n[which, d, side, add] = (part[add] + in_f[which, d, side].astype(F32)).astype(BF16)
                next_copy(which, d, side).start()

    def send_home(step):
        for which in (1, 0):
            d = ORDER_OUT[which][step]
            part = gradient(which, d, pos[which])
            for side in (0, 1):
                arrived(in_n.at[which, d, side], rn5.at[which, d, side])
                part = part + in_n[which, d, side].astype(F32)
            st_z[which, d] = part.astype(BF16)
            owner, dst, copy = z_copy(which, d)
            if d == 0:
                member = (z % 2, (z + 1) % 2)[which]

                @pl.when(owner == c)
                def _():
                    pltpu.make_async_copy(st_z.at[which, d], dst, rz.at[which, member, c]).start()

                @pl.when(owner != c)
                def _():
                    copy.start()
            else:
                copy.start()

    send_far(0)
    send_far(1)
    send_next(0)
    send_far(2)
    send_next(1)
    send_home(0)
    send_far(3)
    send_next(2)
    send_home(1)
    send_next(3)
    send_home(2)
    send_home(3)

    along_z(0, False)
    along_z(3, False)
    for step in range(4):
        if step > 0:
            to_next(step, False)
        to_far(step, False)
    for j in (0, 1):
        give_tile(j).wait_send()
    for copy in stat_copies:
        copy.wait_send()
    give_wp.wait_send()
    give_wq.wait_send()
    for copy in loss_copies:
        copy.wait_send()
    for which in (0, 1):
        for d in range(4):
            for side in (0, 1):
                far_copy(which, d, side).wait_send()
                next_copy(which, d, side).wait_send()

    for slot in range(8):
        pl.when(slot != group)(lambda slot=slot: arrived(losses.at[slot], rl.at[slot]))
    loss = losses[0]
    for slot in range(1, 8):
        loss = loss + losses[slot]
    loss_ref[0, 0] = loss[0, 0] / (32 * BR)

    for which in (0, 1):
        for part in (0, 1):
            for member in (0, 1):
                arrived((in_q, in_p)[which].at[member, :, part * WC:(part + 1) * WC], rz.at[which, member, part])
    for which in (0, 1):
        for d in range(4):
            owner, _, copy = z_copy(which, d)
            if d == 0:
                pl.when(owner != c)(lambda copy=copy: copy.wait_send())
            else:
                copy.wait_send()


def body(queries, passages, pairs):
    dma = pltpu.SemaphoreType.DMA
    loss, in_q, in_p = pl.pallas_call(
        kernel,
        out_shape=(
            jax.ShapeDtypeStruct((1, 1), F32),
            jax.ShapeDtypeStruct((2, *queries.shape), BF16),
            jax.ShapeDtypeStruct((2, *passages.shape), BF16),
        ),
        in_specs=[
            pl.BlockSpec(memory_space=pl.ANY),
            pl.BlockSpec(memory_space=pl.ANY),
            pl.BlockSpec(memory_space=pltpu.SMEM),
        ],
        out_specs=(
            pl.BlockSpec(memory_space=pltpu.SMEM),
            pl.BlockSpec(memory_space=pl.ANY),
            pl.BlockSpec(memory_space=pl.ANY),
        ),
        scratch_shapes=[
            pltpu.VMEM((4, TILE, WC), BF16),
            pltpu.VMEM((4, TILE, WC), BF16),
            pltpu.VMEM((TILE, TILE), F32),
            pltpu.VMEM((CORE, TILE), F32),
            pltpu.VMEM((TILE, TILE), BF16),
            pltpu.VMEM((2, TILE, CORE), BF16),
            pltpu.VMEM((2, 4, BR, WC), BF16),
            pltpu.VMEM((2, 4, 2, HALF, WC), BF16),
            pltpu.VMEM((2, 4, 2, BR, WC), BF16),
            pltpu.VMEM((2, 4, 2, BR, WC), BF16),
            pltpu.VMEM((2, 4, BR, WC), BF16),
            pltpu.VMEM((16, 128), F32),
            pltpu.VMEM((16, 16, 128), F32),
            pltpu.VMEM((8, 128), F32),
            pltpu.VMEM((8, 8, 128), F32),
            dma((2, 4)), dma((2, 4, 2)), dma((2, 2, 2)),
            dma((2, 4, 2)), dma((2, 4, 2)),
            dma((2, 4, 2)), dma((2, 4, 2)),
            dma((2,)), dma((2,)),
            dma((16,)), dma((15,)),
            dma((2,)), dma((2,)),
            dma((2, 4, 2)), dma((2, 4, 2)),
            dma((2, 4, 2)), dma((2, 4, 2)),
            dma((2, 2, 2)), dma((2, 4)),
            dma((8,)), dma((7,)),
        ],
        compiler_params=pltpu.CompilerParams(
            collective_id=0, has_side_effects=True, vmem_limit_bytes=56 * 2**20
        ),
    )(queries, passages, pairs)
    grads = [(pair[0].astype(F32) + pair[1].astype(F32)).astype(BF16) for pair in (in_q, in_p)]
    return loss.reshape(()), *grads


def solution(mesh):
    return jax.shard_map(
        body,
        mesh=mesh,
        in_specs=(P("blk", "wid"), P("blk", "wid"), P()),
        out_specs=(P(), P("blk", "wid"), P("blk", "wid")),
        check_vma=False,
    )
```

```python
import jax
import jax.numpy as jnp
from jax import lax
from jax.experimental import pallas as pl
from jax.experimental.pallas import tpu as pltpu
from jax.sharding import PartitionSpec as P

MESH = pl.DeviceIdType.MESH
BR = 224
HALF = BR // 2
WC = 512
TILE = 4 * BR
CORE = 2 * BR
SUB = 32
NEG = -1e30
SCALE = 4096 ** -0.5
MC = WC // 2
PAIRED = (0, 2, 1, 3)
F32 = jnp.float32
BF16 = jnp.bfloat16


def rows(slot, n=BR, off=0):
    return pl.ds(pl.multiple_of(slot * BR + off, 16), n)


def kernel(
    q_hbm, p_hbm, pairs_ref, loss_ref, in_q, in_p,
    qg, pg, tile, tile_in, wp, wq, st_f, in_f, st_n, in_n, st_z, st_m, in_m, zero, stat, stats, lossv, losses,
    r1, s1, s0, rn, sn, rf, sf, rt, sst, rst, sstat, rw, sw, rf5, sf5, rn5, sn5, rz, sz, rl, sl, rm, sm, rm5, sm5, s_fill,
):
    blk = lax.axis_index("blk")
    z = lax.axis_index("wid")
    x = blk // 8
    y = (blk // 2) % 4
    c = blk % 2
    h = z // 2
    l = ((z + 1) // 2) % 2
    twin = h * 2 + (z + 1) % 2
    flip = 3 - z
    far_x, far_y = (x + 2) % 4, (y + 2) % 4

    def dev(xx, yy, cc, zz):
        return ((xx * 4 + yy) * 2 + cc, zz)

    right = (dev(x, (y + 1) % 4, c, z), dev((x + 1) % 4, y, c, z))
    left = (dev(x, (y + 3) % 4, c, z), dev((x + 3) % 4, y, c, z))
    other = dev(x, y, 1 - c, z)
    gathered = (qg, pg)
    pos = (y, x)

    def remote(src, dst, ssem, rsem, device):
        return pltpu.make_async_remote_copy(
            src_ref=src, dst_ref=dst, send_sem=ssem, recv_sem=rsem, device_id=device, device_id_type=MESH
        )

    def arrived(dst, sem):
        pltpu.make_async_copy(dst, dst, sem).wait()

    barrier = pltpu.get_barrier_semaphore()
    peers = [other]
    for device in (*right, *left):
        peers.append(device)
        peers.append((device[0] + 1 - 2 * c, device[1]))
    for dz in (1, 2, 3):
        for cc in (0, 1):
            peers.append(dev(x, y, cc, (z + dz) % 4))
    for peer in peers:
        pl.semaphore_signal(barrier, inc=1, device_id=peer, device_id_type=MESH)
    pl.semaphore_wait(barrier, len(peers))
    stat_peers = [dev(x, (y + dy) % 4, cc, zz) for dy in (2, 1, 3) for zz in (twin, z) for cc in (0, 1)]
    stat_peers += [dev(x, y, 0, twin), dev(x, y, 1, twin), other]
    loss_peers = [dev(x, y, c, flip)]
    for dx in (1, 2, 3):
        for zz in (z, flip):
            loss_peers.append(dev((x + dx) % 4, y, c, zz))

    turn = 1 - 2 * (z % 2)

    def z_of(which, slot):
        step = (turn, -turn)[which]
        return (z + 4 + (0, -step, step, 2)[slot]) % 4

    def holds(which, zz):
        return zz // 2 if which == 0 else ((zz + 1) // 2) % 2

    def cols(slot, start=0):
        return slice(start + (MC if slot == 3 else 0), start + WC)

    def member(which, zz):
        return (zz % 2, (zz + 1) % 2)[which]

    def lacks(which, one):
        return (holds(which, z) != c) & (member(which, z) == one)

    def fill(start):
        for which in (0, 1):
            for one in (0, 1):

                @pl.when(lacks(which, one))
                def _():
                    for part in (0, 1):
                        dst = (in_q, in_p)[which].at[one, :, part * WC:part * WC + MC]
                        copy = pltpu.make_async_copy(zero, dst, s_fill.at[which, part])
                        copy.start() if start else copy.wait()

    def along_z(slot, start):
        for which in (0, 1):
            zt = z_of(which, slot)

            @pl.when(holds(which, zt) == c)
            def _():
                for part in (0, 1):
                    src = (q_hbm, p_hbm)[which].at[:, cols(slot, part * WC)]
                    dst = gathered[which].at[slot, rows(pos[which]), cols(slot)]
                    copy = remote(src, dst, s1.at[which, slot, part], r1.at[which, slot], dev(x, y, part, zt))
                    if slot == 0:
                        for half in (0, 1):
                            for side, device in ((0, right[which]), (1, left[which])):
                                off = (side, 1 - side)[half] * HALF
                                direct = remote(
                                    (q_hbm, p_hbm)[which].at[off:off + HALF, cols(slot, part * WC)],
                                    gathered[which].at[slot, rows(pos[which], HALF, off), cols(slot)],
                                    s0.at[which, part, side, half], rn.at[which, slot, side, half],
                                    (device[0] - c + part, device[1]),
                                )
                                direct.start() if start else direct.wait_send()
                        if start:
                            @pl.when(c == part)
                            def _():
                                pltpu.make_async_copy(src, dst, r1.at[which, slot]).start()

                        @pl.when(c != part)
                        def _():
                            copy.start() if start else copy.wait_send()
                    else:
                        copy.start() if start else copy.wait_send()

    def to_next(slot, start):
        for which in (0, 1):
            own = gathered[which].at[slot, rows(pos[which]), cols(slot)]
            if start:
                arrived(own, r1.at[which, slot])
            for half in (0, 1):
                for side, device in ((0, right[which]), (1, left[which])):
                    part = gathered[which].at[slot, rows(pos[which], HALF, (side, 1 - side)[half] * HALF), cols(slot)]
                    copy = remote(part, part, sn.at[which, slot, side, half], rn.at[which, slot, side, half], device)
                    copy.start() if start else copy.wait_send()

    def from_next(which, slot, side, half):
        origin = (pos[which] + (3, 1)[side]) % 4
        part = gathered[which].at[slot, rows(origin, HALF, (side, 1 - side)[half] * HALF), cols(slot)]
        return part, rn.at[which, slot, side, half]

    def to_far(slot, start):
        for which in (0, 1):
            for side, device in ((0, right[which]), (1, left[which])):
                part, came = from_next(which, slot, side, 0)
                if start:
                    arrived(part, came)
                copy = remote(part, part, sf.at[which, slot, side], rf.at[which, slot, side], device)
                copy.start() if start else copy.wait_send()

    def rest_of_next(slot):
        for which in (0, 1):
            for side in (0, 1):
                arrived(*from_next(which, slot, side, 1))

    def from_far(slot):
        for which in (0, 1):
            for side in (0, 1):
                far = rows((pos[which] + 2) % 4, HALF, side * HALF)
                arrived(gathered[which].at[slot, far, cols(slot)], rf.at[which, slot, side])

    mates = [dev(x, y, c, z_of(which, 2)) for which in (0, 1)]

    def to_mate(start, steps=(0, 1, 2, 3)):
        for which in (0, 1):
            for step in steps:
                block = (pos[which] + step) % 4
                copy = remote(
                    gathered[which].at[1, rows(block), 0:MC], gathered[which].at[3, rows(block), 0:MC],
                    sm.at[which, block], rm.at[which, block], mates[which],
                )
                copy.start() if start else copy.wait_send()

    def scores(slot, block):
        part = lax.dot_general(
            pg[PAIRED[slot], rows(block), :], qg[slot], (((1,), (1,)), ((), ())), preferred_element_type=F32
        )
        if slot == 0:
            tile[rows(block), :] = part
        else:
            tile[rows(block), :] += part

    def all_scores(slot):
        pl.loop(0, 4)(lambda block: scores(slot, block))

    along_z(0, True)
    along_z(1, True)
    along_z(2, True)
    zero[...] = jnp.zeros((BR, MC), BF16)
    fill(True)
    to_far(0, True)
    to_next(1, True)
    along_z(3, True)
    to_mate(True, (0,))
    to_next(2, True)
    to_far(1, True)
    rest_of_next(1)
    to_mate(True, (1, 3))
    for which in (0, 1):
        arrived(gathered[which].at[0, rows(pos[which])], r1.at[which, 0])
    rest_of_next(0)
    from_far(0)
    all_scores(0)
    to_far(2, True)
    to_next(3, True)
    from_far(1)
    to_mate(True, (2,))
    rest_of_next(2)
    from_far(2)
    all_scores(1)
    to_far(3, True)
    all_scores(2)
    rest_of_next(3)
    from_far(3)
    for which in (0, 1):
        for block in range(4):
            arrived(gathered[which].at[3, rows(block), 0:MC], rm.at[which, block])

    def give_tile(j):
        return remote(
            tile.at[rows(2 * (1 - c) + j)], tile_in.at[pl.ds(j * BR, BR)], sst.at[j], rt.at[j], other
        )

    for j in (0, 1):
        scores(3, 2 * (1 - c) + j)
        give_tile(j).start()
    for j in (0, 1):
        scores(3, 2 * c + j)

    lane = lax.broadcasted_iota(jnp.int32, (1, TILE), 1)
    lanes = lax.broadcasted_iota(jnp.int32, (SUB, TILE), 1)
    subs = lax.broadcasted_iota(jnp.int32, (SUB, TILE), 0)
    eye = lanes - subs

    def diagonal(j):
        return jnp.where((2 * c + j == x) & (h == l), y * BR, -2 * TILE)

    def fold(op, acc, value):
        for k in range(0, SUB, 8):
            acc = op(acc, value[k:k + 8, :])
        return acc

    top = jnp.full((8, TILE), NEG, F32)
    diag = jnp.zeros((8, TILE), F32)
    for j in (0, 1):
        block = ((2 * c + j) * 4 + y) * 2 + l
        allow = None
        for yy in (3, 2, 1, 0):
            mine = (x * 4 + yy) * 2 + h
            flag = jnp.where(mine == block, 1, pairs_ref[mine, block])
            allow = jnp.full((1, TILE), flag, jnp.int32) if allow is None else jnp.where(lane < (yy + 1) * BR, flag, allow)
        allowed = jnp.broadcast_to(allow, (SUB, TILE)) == 1
        start = diagonal(j)
        arrived(tile_in.at[pl.ds(j * BR, BR)], rt.at[j])

        def first(i, carry):
            top, diag = carry
            here = rows(2 * c + j, SUB, i * SUB)
            value = (tile[here, :] + tile_in[pl.ds(pl.multiple_of(j * BR + i * SUB, SUB), SUB), :]) * SCALE
            diag = fold(jnp.add, diag, jnp.where(eye == start + i * SUB, value, 0.0))
            value = jnp.where(allowed, value, NEG)
            tile[here, :] = value
            return fold(jnp.maximum, top, value), diag

        top, diag = lax.fori_loop(0, BR // SUB, first, (top, diag))
    top = jnp.max(top, axis=0, keepdims=True)
    diag = jnp.sum(diag, axis=0, keepdims=True)

    total = jnp.zeros((8, TILE), F32)
    for j in (0, 1):

        def second(i, total):
            here = rows(2 * c + j, SUB, i * SUB)
            value = tile[here, :]
            value = jnp.where(value == NEG, 0.0, jnp.exp(value - top))
            tile[here, :] = value
            return fold(jnp.add, total, value)

        total = lax.fori_loop(0, BR // SUB, second, total)
    total = jnp.sum(total, axis=0, keepdims=True)

    def pack(row):
        parts = [row[:, k * 128:(k + 1) * 128] for k in range(TILE // 128)]
        return jnp.concatenate(parts + [jnp.zeros((1, 128), F32)], axis=0)

    def unpack(block):
        return jnp.concatenate([block[k:k + 1, :] for k in range(TILE // 128)], axis=1)

    mine = (y * 2 + l) * 2 + c
    stat[0:8, :] = pack(jnp.where(total > 0, top + jnp.log(total), NEG))
    stat[8:16, :] = pack(diag)
    stats[mine] = stat[...]
    stat_copies = [
        remote(stat, stats.at[mine], sstat.at[i], rst.at[mine], peer) for i, peer in enumerate(stat_peers)
    ]
    for copy in stat_copies:
        copy.start()
    for slot in range(16):
        pl.when(slot != mine)(lambda slot=slot: arrived(stats.at[slot], rst.at[slot]))
    highest = stats[0, 0:8, :]
    for slot in range(1, 16):
        highest = jnp.maximum(highest, stats[slot, 0:8, :])
    totals = jnp.zeros((8, 128), F32)
    positive = jnp.zeros((8, 128), F32)
    for slot in range(16):
        totals = totals + jnp.exp(stats[slot, 0:8, :] - highest)
        positive = positive + stats[slot, 8:16, :]
    log_total = highest + jnp.log(totals)
    factor = jnp.exp(top - unpack(log_total))

    def give_wp(j):
        part = wp.at[rows(2 * c + j)]
        return remote(part, part, sw.at[j], rw.at[j], other)

    for j in (0, 1):
        start = diagonal(j)

        def third(i, _):
            here = rows(2 * c + j, SUB, i * SUB)
            value = tile[here, :] * factor - jnp.where(eye == start + i * SUB, 1.0, 0.0)
            wp[here, :] = value.astype(BF16)
            return _

        lax.fori_loop(0, BR // SUB, third, 0)
        give_wp(j).start()
    my_rows = pl.ds(pl.multiple_of(c * CORE, CORE), CORE)
    wq[c] = jnp.transpose(wp[my_rows, :])
    give_wq = remote(wq.at[c], wq.at[c], sw.at[2], rw.at[2], other)
    give_wq.start()

    group = x * 2 + h
    row = lax.broadcasted_iota(jnp.int32, (8, 128), 0)
    lossv[...] = jnp.full((8, 128), jnp.sum(jnp.where(row < TILE // 128, log_total - positive, 0.0)), F32)
    losses[group] = lossv[...]
    loss_copies = [
        remote(lossv, losses.at[group], sl.at[i], rl.at[group], peer) for i, peer in enumerate(loss_peers)
    ]
    for copy in loss_copies:
        copy.start()

    for j in (0, 1):
        arrived(wp.at[rows(2 * (1 - c) + j)], rw.at[j])

    def gradient(which, slot, block, span):
        if which == 1:
            return jnp.dot(wp[rows(block), :], qg[PAIRED[slot], :, span], preferred_element_type=F32)
        return jnp.dot(wq[0, rows(block), :], pg[PAIRED[slot], 0:CORE, span], preferred_element_type=F32) + jnp.dot(
            wq[1, rows(block), :], pg[PAIRED[slot], CORE:TILE, span], preferred_element_type=F32
        )

    def total_of(which, slot, block):
        part = gradient(which, slot, block, cols(slot))
        if slot == 1:
            arrived(in_m.at[which, block], rm5.at[which, block])
            part = jnp.concatenate([part[:, 0:MC] + in_m[which, block].astype(F32), part[:, MC:WC]], axis=1)
        return part

    def far_copy(which, slot, side):
        return remote(
            st_f.at[which, slot, pl.ds(side * HALF, HALF), cols(slot)], in_f.at[which, slot, side, :, cols(slot)],
            sf5.at[which, slot, side], rf5.at[which, slot, side], (right, left)[side][which],
        )

    def next_copy(which, slot, side, half):
        off = (1 - side, side)[half] * HALF
        return remote(
            st_n.at[which, slot, side, pl.ds(off, HALF), cols(slot)],
            in_n.at[which, slot, side, pl.ds(off, HALF), cols(slot)],
            sn5.at[which, slot, side, half], rn5.at[which, slot, side, half], (right, left)[side][which],
        )

    def mate_copy(which, block):
        return remote(
            st_m.at[which, block], in_m.at[which, block], sm5.at[which, block], rm5.at[which, block], mates[which]
        )

    def z_copy(which, slot):
        owner = holds(which, z)
        first = c * WC + (MC if slot == 3 else 0)
        span = pl.ds(pl.multiple_of(first, MC), WC - MC if slot == 3 else WC)
        dst = (in_q, in_p)[which].at[member(which, z), :, span]
        return owner, dst, remote(
            st_z.at[which, slot, :, cols(slot)], dst, sz.at[which, slot], rz.at[which, member(which, z), c],
            dev(x, y, owner, z_of(which, slot)),
        )

    def send_mate():
        for which in (1, 0):
            for step in (2, 1, 3, 0):
                block = (pos[which] + step) % 4
                st_m[which, block] = gradient(which, 3, block, slice(0, MC)).astype(BF16)
                mate_copy(which, block).start()

    def send_far(slot):
        for which in (1, 0):
            if which == 0 and slot == 2:
                arrived(wq.at[1 - c], rw.at[2])
            st_f[which, slot, :, cols(slot)] = total_of(which, slot, (pos[which] + 2) % 4).astype(BF16)
            for side in (0, 1):
                far_copy(which, slot, side).start()

    def send_next(slot):
        for which in (1, 0):
            for side in (0, 1):
                part = total_of(which, slot, (pos[which] + (1, 3)[side]) % 4)
                add, keep = slice(side * HALF, (side + 1) * HALF), slice((1 - side) * HALF, (2 - side) * HALF)
                st_n[which, slot, side, keep, cols(slot)] = part[keep].astype(BF16)
                next_copy(which, slot, side, 0).start()
                arrived(in_f.at[which, slot, side, :, cols(slot)], rf5.at[which, slot, side])
                st_n[which, slot, side, add, cols(slot)] = (
                    part[add] + in_f[which, slot, side, :, cols(slot)].astype(F32)
                ).astype(BF16)
                next_copy(which, slot, side, 1).start()

    def send_home(slot):
        for which in (1, 0):
            part = total_of(which, slot, pos[which])
            for side in (0, 1):
                for half in (0, 1):
                    off = (1 - side, side)[half] * HALF
                    arrived(in_n.at[which, slot, side, pl.ds(off, HALF), cols(slot)], rn5.at[which, slot, side, half])
                part = part + in_n[which, slot, side, :, cols(slot)].astype(F32)
            st_z[which, slot, :, cols(slot)] = part.astype(BF16)
            owner, dst, copy = z_copy(which, slot)
            if slot == 0:

                @pl.when(owner == c)
                def _():
                    pltpu.make_async_copy(st_z.at[which, slot], dst, rz.at[which, member(which, z), c]).start()

                @pl.when(owner != c)
                def _():
                    copy.start()
            else:
                copy.start()

    send_far(2)
    send_far(3)
    send_far(0)
    send_mate()
    send_next(2)
    send_next(3)
    send_far(1)
    send_home(2)
    send_next(1)
    send_home(3)
    send_next(0)
    send_home(1)
    send_home(0)

    to_mate(False)
    for slot in range(4):
        along_z(slot, False)
        if slot > 0:
            to_next(slot, False)
        to_far(slot, False)
    for j in (0, 1):
        give_tile(j).wait_send()
    for copy in stat_copies:
        copy.wait_send()
    for j in (0, 1):
        give_wp(j).wait_send()
    give_wq.wait_send()
    for copy in loss_copies:
        copy.wait_send()
    for which in (0, 1):
        for slot in range(4):
            mate_copy(which, slot).wait_send()
            for side in (0, 1):
                far_copy(which, slot, side).wait_send()
                for half in (0, 1):
                    next_copy(which, slot, side, half).wait_send()

    for slot in range(8):
        pl.when(slot != group)(lambda slot=slot: arrived(losses.at[slot], rl.at[slot]))
    loss = losses[0]
    for slot in range(1, 8):
        loss = loss + losses[slot]
    loss_ref[0, 0] = loss[0, 0] / (32 * BR)

    for which in (0, 1):
        for part in (0, 1):
            for one in (0, 1):
                whole = (in_q, in_p)[which].at[one, :, part * WC:(part + 1) * WC]
                rest = (in_q, in_p)[which].at[one, :, cols(3, part * WC)]
                half = lacks(which, one)
                pl.when(half)(lambda rest=rest, one=one, part=part, which=which: arrived(rest, rz.at[which, one, part]))
                pl.when(jnp.logical_not(half))(
                    lambda whole=whole, one=one, part=part, which=which: arrived(whole, rz.at[which, one, part])
                )
    fill(False)
    for which in (0, 1):
        for slot in range(4):
            owner, _, copy = z_copy(which, slot)
            if slot == 0:
                pl.when(owner != c)(lambda copy=copy: copy.wait_send())
            else:
                copy.wait_send()


def body(queries, passages, pairs):
    dma = pltpu.SemaphoreType.DMA
    loss, in_q, in_p = pl.pallas_call(
        kernel,
        out_shape=(
            jax.ShapeDtypeStruct((1, 1), F32),
            jax.ShapeDtypeStruct((2, *queries.shape), BF16),
            jax.ShapeDtypeStruct((2, *passages.shape), BF16),
        ),
        in_specs=[
            pl.BlockSpec(memory_space=pl.ANY),
            pl.BlockSpec(memory_space=pl.ANY),
            pl.BlockSpec(memory_space=pltpu.SMEM),
        ],
        out_specs=(
            pl.BlockSpec(memory_space=pltpu.SMEM),
            pl.BlockSpec(memory_space=pl.ANY),
            pl.BlockSpec(memory_space=pl.ANY),
        ),
        scratch_shapes=[
            pltpu.VMEM((4, TILE, WC), BF16),
            pltpu.VMEM((4, TILE, WC), BF16),
            pltpu.VMEM((TILE, TILE), F32),
            pltpu.VMEM((CORE, TILE), F32),
            pltpu.VMEM((TILE, TILE), BF16),
            pltpu.VMEM((2, TILE, CORE), BF16),
            pltpu.VMEM((2, 4, BR, WC), BF16),
            pltpu.VMEM((2, 4, 2, HALF, WC), BF16),
            pltpu.VMEM((2, 4, 2, BR, WC), BF16),
            pltpu.VMEM((2, 4, 2, BR, WC), BF16),
            pltpu.VMEM((2, 4, BR, WC), BF16),
            pltpu.VMEM((2, 4, BR, MC), BF16),
            pltpu.VMEM((2, 4, BR, MC), BF16),
            pltpu.VMEM((BR, MC), BF16),
            pltpu.VMEM((16, 128), F32),
            pltpu.VMEM((16, 16, 128), F32),
            pltpu.VMEM((8, 128), F32),
            pltpu.VMEM((8, 8, 128), F32),
            dma((2, 4)), dma((2, 4, 2)), dma((2, 2, 2, 2)),
            dma((2, 4, 2, 2)), dma((2, 4, 2, 2)),
            dma((2, 4, 2)), dma((2, 4, 2)),
            dma((2,)), dma((2,)),
            dma((16,)), dma((15,)),
            dma((3,)), dma((3,)),
            dma((2, 4, 2)), dma((2, 4, 2)),
            dma((2, 4, 2, 2)), dma((2, 4, 2, 2)),
            dma((2, 2, 2)), dma((2, 4)),
            dma((8,)), dma((7,)),
            dma((2, 4)), dma((2, 4)),
            dma((2, 4)), dma((2, 4)),
            dma((2, 2)),
        ],
        compiler_params=pltpu.CompilerParams(
            collective_id=0, has_side_effects=True, vmem_limit_bytes=56 * 2**20
        ),
    )(queries, passages, pairs)
    grads = [(pair[0].astype(F32) + pair[1].astype(F32)).astype(BF16) for pair in (in_q, in_p)]
    return loss.reshape(()), *grads


def solution(mesh):
    return jax.shard_map(
        body,
        mesh=mesh,
        in_specs=(P("blk", "wid"), P("blk", "wid"), P()),
        out_specs=(P(), P("blk", "wid"), P("blk", "wid")),
        check_vma=False,
    )
```

```python
import jax
import jax.numpy as jnp
from jax import lax
from jax.experimental import pallas as pl
from jax.experimental.pallas import tpu as pltpu
from jax.sharding import PartitionSpec as P

MESH = pl.DeviceIdType.MESH
BR = 224
HALF = BR // 2
WC = 512
TILE = 4 * BR
CORE = 2 * BR
SUB = 32
NEG = -1e30
SCALE = 4096 ** -0.5
MC = 384
PAIRED = (0, 2, 1, 3)
F32 = jnp.float32
BF16 = jnp.bfloat16


def rows(slot, n=BR, off=0):
    return pl.ds(pl.multiple_of(slot * BR + off, 16), n)


def kernel(
    q_hbm, p_hbm, pairs_ref, loss_ref, in_q, in_p,
    qg, pg, tile, tile_in, wp, wq, st_f, in_f, st_n, in_n, st_z, st_m, in_m, zero, stat, stats, lossv, losses,
    r1, s1, s0, rn, sn, rf, sf, rt, sst, rst, sstat, rw, sw, rf5, sf5, rn5, sn5, rz, sz, rl, sl, rm, sm, rm5, sm5, s_fill,
):
    blk = lax.axis_index("blk")
    z = lax.axis_index("wid")
    x = blk // 8
    y = (blk // 2) % 4
    c = blk % 2
    h = z // 2
    l = ((z + 1) // 2) % 2
    twin = h * 2 + (z + 1) % 2
    flip = 3 - z
    far_x, far_y = (x + 2) % 4, (y + 2) % 4

    def dev(xx, yy, cc, zz):
        return ((xx * 4 + yy) * 2 + cc, zz)

    right = (dev(x, (y + 1) % 4, c, z), dev((x + 1) % 4, y, c, z))
    left = (dev(x, (y + 3) % 4, c, z), dev((x + 3) % 4, y, c, z))
    other = dev(x, y, 1 - c, z)
    gathered = (qg, pg)
    pos = (y, x)

    def remote(src, dst, ssem, rsem, device):
        return pltpu.make_async_remote_copy(
            src_ref=src, dst_ref=dst, send_sem=ssem, recv_sem=rsem, device_id=device, device_id_type=MESH
        )

    def arrived(dst, sem):
        pltpu.make_async_copy(dst, dst, sem).wait()

    barrier = pltpu.get_barrier_semaphore()
    peers = [other]
    for device in (*right, *left):
        peers.append(device)
        peers.append((device[0] + 1 - 2 * c, device[1]))
    for dz in (1, 2, 3):
        for cc in (0, 1):
            peers.append(dev(x, y, cc, (z + dz) % 4))
    for peer in peers:
        pl.semaphore_signal(barrier, inc=1, device_id=peer, device_id_type=MESH)
    pl.semaphore_wait(barrier, len(peers))
    stat_peers = [dev(x, (y + dy) % 4, cc, zz) for dy in (2, 1, 3) for zz in (twin, z) for cc in (0, 1)]
    stat_peers += [dev(x, y, 0, twin), dev(x, y, 1, twin), other]
    loss_peers = [dev(x, y, c, flip)]
    for dx in (1, 2, 3):
        for zz in (z, flip):
            loss_peers.append(dev((x + dx) % 4, y, c, zz))

    turn = 1 - 2 * (z % 2)

    def z_of(which, slot):
        step = (turn, -turn)[which]
        return (z + 4 + (0, -step, step, 2)[slot]) % 4

    def holds(which, zz):
        return zz // 2 if which == 0 else ((zz + 1) // 2) % 2

    def cols(slot, start=0):
        return slice(start + (MC if slot == 3 else 0), start + WC)

    def member(which, zz):
        return (zz % 2, (zz + 1) % 2)[which]

    def lacks(which, one):
        return (holds(which, z) != c) & (member(which, z) == one)

    def fill(start):
        for which in (0, 1):
            for one in (0, 1):

                @pl.when(lacks(which, one))
                def _():
                    for part in (0, 1):
                        dst = (in_q, in_p)[which].at[one, :, part * WC:part * WC + MC]
                        copy = pltpu.make_async_copy(zero, dst, s_fill.at[which, part])
                        copy.start() if start else copy.wait()

    def along_z(slot, start):
        for which in (0, 1):
            zt = z_of(which, slot)

            @pl.when(holds(which, zt) == c)
            def _():
                for part in (0, 1):
                    src = (q_hbm, p_hbm)[which].at[:, cols(slot, part * WC)]
                    dst = gathered[which].at[slot, rows(pos[which]), cols(slot)]
                    copy = remote(src, dst, s1.at[which, slot, part], r1.at[which, slot], dev(x, y, part, zt))
                    if slot == 0:
                        for half in (0, 1):
                            for side, device in ((0, right[which]), (1, left[which])):
                                off = (side, 1 - side)[half] * HALF
                                direct = remote(
                                    (q_hbm, p_hbm)[which].at[off:off + HALF, cols(slot, part * WC)],
                                    gathered[which].at[slot, rows(pos[which], HALF, off), cols(slot)],
                                    s0.at[which, part, side, half], rn.at[which, slot, side, half],
                                    (device[0] - c + part, device[1]),
                                )
                                direct.start() if start else direct.wait_send()
                        if start:
                            @pl.when(c == part)
                            def _():
                                pltpu.make_async_copy(src, dst, r1.at[which, slot]).start()

                        @pl.when(c != part)
                        def _():
                            copy.start() if start else copy.wait_send()
                    else:
                        copy.start() if start else copy.wait_send()

    def to_next(slot, start):
        for which in (0, 1):
            own = gathered[which].at[slot, rows(pos[which]), cols(slot)]
            if start:
                arrived(own, r1.at[which, slot])
            for half in (0, 1):
                for side, device in ((0, right[which]), (1, left[which])):
                    part = gathered[which].at[slot, rows(pos[which], HALF, (side, 1 - side)[half] * HALF), cols(slot)]
                    copy = remote(part, part, sn.at[which, slot, side, half], rn.at[which, slot, side, half], device)
                    copy.start() if start else copy.wait_send()

    def from_next(which, slot, side, half):
        origin = (pos[which] + (3, 1)[side]) % 4
        part = gathered[which].at[slot, rows(origin, HALF, (side, 1 - side)[half] * HALF), cols(slot)]
        return part, rn.at[which, slot, side, half]

    def to_far(slot, start):
        for which in (0, 1):
            for side, device in ((0, right[which]), (1, left[which])):
                part, came = from_next(which, slot, side, 0)
                if start:
                    arrived(part, came)
                copy = remote(part, part, sf.at[which, slot, side], rf.at[which, slot, side], device)
                copy.start() if start else copy.wait_send()

    def rest_of_next(slot):
        for which in (0, 1):
            for side in (0, 1):
                arrived(*from_next(which, slot, side, 1))

    def from_far(slot):
        for which in (0, 1):
            for side in (0, 1):
                far = rows((pos[which] + 2) % 4, HALF, side * HALF)
                arrived(gathered[which].at[slot, far, cols(slot)], rf.at[which, slot, side])

    mates = [dev(x, y, c, z_of(which, 2)) for which in (0, 1)]

    def to_mate(start, steps=(0, 1, 2, 3)):
        for which in (0, 1):
            for step in steps:
                block = (pos[which] + step) % 4
                copy = remote(
                    gathered[which].at[1, rows(block), 0:MC], gathered[which].at[3, rows(block), 0:MC],
                    sm.at[which, block], rm.at[which, block], mates[which],
                )
                copy.start() if start else copy.wait_send()

    def scores(slot, block):
        part = lax.dot_general(
            pg[PAIRED[slot], rows(block), :], qg[slot], (((1,), (1,)), ((), ())), preferred_element_type=F32
        )
        if slot == 0:
            tile[rows(block), :] = part
        else:
            tile[rows(block), :] += part

    def all_scores(slot):
        pl.loop(0, 4)(lambda block: scores(slot, block))

    along_z(0, True)
    along_z(1, True)
    along_z(2, True)
    zero[...] = jnp.zeros((BR, MC), BF16)
    fill(True)
    to_far(0, True)
    to_next(1, True)
    along_z(3, True)
    to_mate(True, (0,))
    to_next(2, True)
    to_far(1, True)
    rest_of_next(1)
    to_mate(True, (1, 3))
    for which in (0, 1):
        arrived(gathered[which].at[0, rows(pos[which])], r1.at[which, 0])
    rest_of_next(0)
    from_far(0)
    all_scores(0)
    to_far(2, True)
    to_next(3, True)
    from_far(1)
    to_mate(True, (2,))
    rest_of_next(2)
    from_far(2)
    all_scores(1)
    to_far(3, True)
    all_scores(2)
    rest_of_next(3)
    from_far(3)
    for which in (0, 1):
        for block in range(4):
            arrived(gathered[which].at[3, rows(block), 0:MC], rm.at[which, block])

    def give_tile(j):
        return remote(
            tile.at[rows(2 * (1 - c) + j)], tile_in.at[pl.ds(j * BR, BR)], sst.at[j], rt.at[j], other
        )

    for j in (0, 1):
        scores(3, 2 * (1 - c) + j)
        give_tile(j).start()
    for j in (0, 1):
        scores(3, 2 * c + j)

    lane = lax.broadcasted_iota(jnp.int32, (1, TILE), 1)
    lanes = lax.broadcasted_iota(jnp.int32, (SUB, TILE), 1)
    subs = lax.broadcasted_iota(jnp.int32, (SUB, TILE), 0)
    eye = lanes - subs

    def diagonal(j):
        return jnp.where((2 * c + j == x) & (h == l), y * BR, -2 * TILE)

    def fold(op, acc, value):
        for k in range(0, SUB, 8):
            acc = op(acc, value[k:k + 8, :])
        return acc

    top = jnp.full((8, TILE), NEG, F32)
    diag = jnp.zeros((8, TILE), F32)
    for j in (0, 1):
        block = ((2 * c + j) * 4 + y) * 2 + l
        allow = None
        for yy in (3, 2, 1, 0):
            mine = (x * 4 + yy) * 2 + h
            flag = jnp.where(mine == block, 1, pairs_ref[mine, block])
            allow = jnp.full((1, TILE), flag, jnp.int32) if allow is None else jnp.where(lane < (yy + 1) * BR, flag, allow)
        allowed = jnp.broadcast_to(allow, (SUB, TILE)) == 1
        start = diagonal(j)
        arrived(tile_in.at[pl.ds(j * BR, BR)], rt.at[j])

        def first(i, carry):
            top, diag = carry
            here = rows(2 * c + j, SUB, i * SUB)
            value = (tile[here, :] + tile_in[pl.ds(pl.multiple_of(j * BR + i * SUB, SUB), SUB), :]) * SCALE
            diag = fold(jnp.add, diag, jnp.where(eye == start + i * SUB, value, 0.0))
            value = jnp.where(allowed, value, NEG)
            tile[here, :] = value
            return fold(jnp.maximum, top, value), diag

        top, diag = lax.fori_loop(0, BR // SUB, first, (top, diag))
    top = jnp.max(top, axis=0, keepdims=True)
    diag = jnp.sum(diag, axis=0, keepdims=True)

    total = jnp.zeros((8, TILE), F32)
    for j in (0, 1):

        def second(i, total):
            here = rows(2 * c + j, SUB, i * SUB)
            value = tile[here, :]
            value = jnp.where(value == NEG, 0.0, jnp.exp(value - top))
            tile[here, :] = value
            return fold(jnp.add, total, value)

        total = lax.fori_loop(0, BR // SUB, second, total)
    total = jnp.sum(total, axis=0, keepdims=True)

    def pack(row):
        parts = [row[:, k * 128:(k + 1) * 128] for k in range(TILE // 128)]
        return jnp.concatenate(parts + [jnp.zeros((1, 128), F32)], axis=0)

    def unpack(block):
        return jnp.concatenate([block[k:k + 1, :] for k in range(TILE // 128)], axis=1)

    mine = (y * 2 + l) * 2 + c
    stat[0:8, :] = pack(jnp.where(total > 0, top + jnp.log(total), NEG))
    stat[8:16, :] = pack(diag)
    stats[mine] = stat[...]
    stat_copies = [
        remote(stat, stats.at[mine], sstat.at[i], rst.at[mine], peer) for i, peer in enumerate(stat_peers)
    ]
    for copy in stat_copies:
        copy.start()
    for slot in range(16):
        pl.when(slot != mine)(lambda slot=slot: arrived(stats.at[slot], rst.at[slot]))
    highest = stats[0, 0:8, :]
    for slot in range(1, 16):
        highest = jnp.maximum(highest, stats[slot, 0:8, :])
    totals = jnp.zeros((8, 128), F32)
    positive = jnp.zeros((8, 128), F32)
    for slot in range(16):
        totals = totals + jnp.exp(stats[slot, 0:8, :] - highest)
        positive = positive + stats[slot, 8:16, :]
    log_total = highest + jnp.log(totals)
    factor = jnp.exp(top - unpack(log_total))

    def give_wp(j):
        part = wp.at[rows(2 * c + j)]
        return remote(part, part, sw.at[j], rw.at[j], other)

    for j in (0, 1):
        start = diagonal(j)

        def third(i, _):
            here = rows(2 * c + j, SUB, i * SUB)
            value = tile[here, :] * factor - jnp.where(eye == start + i * SUB, 1.0, 0.0)
            wp[here, :] = value.astype(BF16)
            return _

        lax.fori_loop(0, BR // SUB, third, 0)
        give_wp(j).start()
    my_rows = pl.ds(pl.multiple_of(c * CORE, CORE), CORE)
    wq[c] = jnp.transpose(wp[my_rows, :])

    group = x * 2 + h
    row = lax.broadcasted_iota(jnp.int32, (8, 128), 0)
    lossv[...] = jnp.full((8, 128), jnp.sum(jnp.where(row < TILE // 128, log_total - positive, 0.0)), F32)
    losses[group] = lossv[...]
    loss_copies = [
        remote(lossv, losses.at[group], sl.at[i], rl.at[group], peer) for i, peer in enumerate(loss_peers)
    ]
    for copy in loss_copies:
        copy.start()

    for j in (0, 1):
        arrived(wp.at[rows(2 * (1 - c) + j)], rw.at[j])

    def gradient(which, slot, block, span):
        if which == 1:
            return jnp.dot(wp[rows(block), :], qg[PAIRED[slot], :, span], preferred_element_type=F32)
        return jnp.dot(wq[0, rows(block), :], pg[PAIRED[slot], 0:CORE, span], preferred_element_type=F32) + jnp.dot(
            wq[1, rows(block), :], pg[PAIRED[slot], CORE:TILE, span], preferred_element_type=F32
        )

    def total_of(which, slot, block):
        part = gradient(which, slot, block, cols(slot))
        if slot == 1:
            arrived(in_m.at[which, block], rm5.at[which, block])
            part = jnp.concatenate([part[:, 0:MC] + in_m[which, block].astype(F32), part[:, MC:WC]], axis=1)
        return part

    def far_copy(which, slot, side):
        return remote(
            st_f.at[which, slot, pl.ds(side * HALF, HALF), cols(slot)], in_f.at[which, slot, side, :, cols(slot)],
            sf5.at[which, slot, side], rf5.at[which, slot, side], (right, left)[side][which],
        )

    def next_copy(which, slot, side, half):
        off = (1 - side, side)[half] * HALF
        return remote(
            st_n.at[which, slot, side, pl.ds(off, HALF), cols(slot)],
            in_n.at[which, slot, side, pl.ds(off, HALF), cols(slot)],
            sn5.at[which, slot, side, half], rn5.at[which, slot, side, half], (right, left)[side][which],
        )

    def mate_copy(which, block):
        return remote(
            st_m.at[which, block], in_m.at[which, block], sm5.at[which, block], rm5.at[which, block], mates[which]
        )

    def z_copy(which, slot):
        owner = holds(which, z)
        first = c * WC + (MC if slot == 3 else 0)
        span = pl.ds(pl.multiple_of(first, 128), WC - MC if slot == 3 else WC)
        dst = (in_q, in_p)[which].at[member(which, z), :, span]
        return owner, dst, remote(
            st_z.at[which, slot, :, cols(slot)], dst, sz.at[which, slot], rz.at[which, member(which, z), c],
            dev(x, y, owner, z_of(which, slot)),
        )

    def send_mate():
        for which in (1, 0):
            for step in (2, 1, 3, 0):
                block = (pos[which] + step) % 4
                st_m[which, block] = gradient(which, 3, block, slice(0, MC)).astype(BF16)
                mate_copy(which, block).start()

    def send_far(slot):
        for which in (1, 0):
            if which == 0 and slot == 2:
                wq[1 - c] = jnp.transpose(wp[pl.ds(pl.multiple_of((1 - c) * CORE, CORE), CORE), :])
            st_f[which, slot, :, cols(slot)] = total_of(which, slot, (pos[which] + 2) % 4).astype(BF16)
            for side in (0, 1):
                far_copy(which, slot, side).start()

    def send_next(slot):
        for which in (1, 0):
            for side in (0, 1):
                part = total_of(which, slot, (pos[which] + (1, 3)[side]) % 4)
                add, keep = slice(side * HALF, (side + 1) * HALF), slice((1 - side) * HALF, (2 - side) * HALF)
                st_n[which, slot, side, keep, cols(slot)] = part[keep].astype(BF16)
                next_copy(which, slot, side, 0).start()
                arrived(in_f.at[which, slot, side, :, cols(slot)], rf5.at[which, slot, side])
                st_n[which, slot, side, add, cols(slot)] = (
                    part[add] + in_f[which, slot, side, :, cols(slot)].astype(F32)
                ).astype(BF16)
                next_copy(which, slot, side, 1).start()

    def send_home(slot):
        for which in (1, 0):
            part = total_of(which, slot, pos[which])
            for side in (0, 1):
                for half in (0, 1):
                    off = (1 - side, side)[half] * HALF
                    arrived(in_n.at[which, slot, side, pl.ds(off, HALF), cols(slot)], rn5.at[which, slot, side, half])
                part = part + in_n[which, slot, side, :, cols(slot)].astype(F32)
            st_z[which, slot, :, cols(slot)] = part.astype(BF16)
            owner, dst, copy = z_copy(which, slot)
            if slot == 0:

                @pl.when(owner == c)
                def _():
                    pltpu.make_async_copy(st_z.at[which, slot], dst, rz.at[which, member(which, z), c]).start()

                @pl.when(owner != c)
                def _():
                    copy.start()
            else:
                copy.start()

    send_far(2)
    send_far(3)
    send_far(0)
    send_mate()
    send_next(2)
    send_next(3)
    send_far(1)
    send_home(2)
    send_next(1)
    send_home(3)
    send_next(0)
    send_home(1)
    send_home(0)

    to_mate(False)
    for slot in range(4):
        along_z(slot, False)
        if slot > 0:
            to_next(slot, False)
        to_far(slot, False)
    for j in (0, 1):
        give_tile(j).wait_send()
    for copy in stat_copies:
        copy.wait_send()
    for j in (0, 1):
        give_wp(j).wait_send()
    for copy in loss_copies:
        copy.wait_send()
    for which in (0, 1):
        for slot in range(4):
            mate_copy(which, slot).wait_send()
            for side in (0, 1):
                far_copy(which, slot, side).wait_send()
                for half in (0, 1):
                    next_copy(which, slot, side, half).wait_send()

    for slot in range(8):
        pl.when(slot != group)(lambda slot=slot: arrived(losses.at[slot], rl.at[slot]))
    loss = losses[0]
    for slot in range(1, 8):
        loss = loss + losses[slot]
    loss_ref[0, 0] = loss[0, 0] / (32 * BR)

    for which in (0, 1):
        for part in (0, 1):
            for one in (0, 1):
                whole = (in_q, in_p)[which].at[one, :, part * WC:(part + 1) * WC]
                rest = (in_q, in_p)[which].at[one, :, cols(3, part * WC)]
                half = lacks(which, one)
                pl.when(half)(lambda rest=rest, one=one, part=part, which=which: arrived(rest, rz.at[which, one, part]))
                pl.when(jnp.logical_not(half))(
                    lambda whole=whole, one=one, part=part, which=which: arrived(whole, rz.at[which, one, part])
                )
    fill(False)
    for which in (0, 1):
        for slot in range(4):
            owner, _, copy = z_copy(which, slot)
            if slot == 0:
                pl.when(owner != c)(lambda copy=copy: copy.wait_send())
            else:
                copy.wait_send()


def body(queries, passages, pairs):
    dma = pltpu.SemaphoreType.DMA
    loss, in_q, in_p = pl.pallas_call(
        kernel,
        out_shape=(
            jax.ShapeDtypeStruct((1, 1), F32),
            jax.ShapeDtypeStruct((2, *queries.shape), BF16),
            jax.ShapeDtypeStruct((2, *passages.shape), BF16),
        ),
        in_specs=[
            pl.BlockSpec(memory_space=pl.ANY),
            pl.BlockSpec(memory_space=pl.ANY),
            pl.BlockSpec(memory_space=pltpu.SMEM),
        ],
        out_specs=(
            pl.BlockSpec(memory_space=pltpu.SMEM),
            pl.BlockSpec(memory_space=pl.ANY),
            pl.BlockSpec(memory_space=pl.ANY),
        ),
        scratch_shapes=[
            pltpu.VMEM((4, TILE, WC), BF16),
            pltpu.VMEM((4, TILE, WC), BF16),
            pltpu.VMEM((TILE, TILE), F32),
            pltpu.VMEM((CORE, TILE), F32),
            pltpu.VMEM((TILE, TILE), BF16),
            pltpu.VMEM((2, TILE, CORE), BF16),
            pltpu.VMEM((2, 4, BR, WC), BF16),
            pltpu.VMEM((2, 4, 2, HALF, WC), BF16),
            pltpu.VMEM((2, 4, 2, BR, WC), BF16),
            pltpu.VMEM((2, 4, 2, BR, WC), BF16),
            pltpu.VMEM((2, 4, BR, WC), BF16),
            pltpu.VMEM((2, 4, BR, MC), BF16),
            pltpu.VMEM((2, 4, BR, MC), BF16),
            pltpu.VMEM((BR, MC), BF16),
            pltpu.VMEM((16, 128), F32),
            pltpu.VMEM((16, 16, 128), F32),
            pltpu.VMEM((8, 128), F32),
            pltpu.VMEM((8, 8, 128), F32),
            dma((2, 4)), dma((2, 4, 2)), dma((2, 2, 2, 2)),
            dma((2, 4, 2, 2)), dma((2, 4, 2, 2)),
            dma((2, 4, 2)), dma((2, 4, 2)),
            dma((2,)), dma((2,)),
            dma((16,)), dma((15,)),
            dma((2,)), dma((2,)),
            dma((2, 4, 2)), dma((2, 4, 2)),
            dma((2, 4, 2, 2)), dma((2, 4, 2, 2)),
            dma((2, 2, 2)), dma((2, 4)),
            dma((8,)), dma((7,)),
            dma((2, 4)), dma((2, 4)),
            dma((2, 4)), dma((2, 4)),
            dma((2, 2)),
        ],
        compiler_params=pltpu.CompilerParams(
            collective_id=0, has_side_effects=True, vmem_limit_bytes=56 * 2**20
        ),
    )(queries, passages, pairs)
    grads = [(pair[0].astype(F32) + pair[1].astype(F32)).astype(BF16) for pair in (in_q, in_p)]
    return loss.reshape(()), *grads


def solution(mesh):
    return jax.shard_map(
        body,
        mesh=mesh,
        in_specs=(P("blk", "wid"), P("blk", "wid"), P()),
        out_specs=(P(), P("blk", "wid"), P("blk", "wid")),
        check_vma=False,
    )
```

```python
import jax
import jax.numpy as jnp
from jax import lax
from jax.experimental import pallas as pl
from jax.experimental.pallas import tpu as pltpu
from jax.sharding import PartitionSpec as P

MESH = pl.DeviceIdType.MESH
BR = 224
HALF = BR // 2
WC = 512
TILE = 4 * BR
CORE = 2 * BR
SUB = 32
NEG = -1e30
SCALE = 4096 ** -0.5
MC = 384
PAIRED = (0, 2, 1, 3)
F32 = jnp.float32
BF16 = jnp.bfloat16


def rows(slot, n=BR, off=0):
    return pl.ds(pl.multiple_of(slot * BR + off, 16), n)


def kernel(
    q_hbm, p_hbm, pairs_ref, loss_ref, in_q, in_p,
    qg, pg, tile, tile_in, wp, wq, st_f, in_f, st_n, in_n, st_z, st_m, in_m, zero, stat, stats, lossv, losses,
    r1, s1, s0, rn, sn, rf, sf, rt, sst, rst, sstat, rw, sw, rf5, sf5, rn5, sn5, rz, sz, rl, sl, rm, sm, rm5, sm5, s_fill,
):
    blk = lax.axis_index("blk")
    z = lax.axis_index("wid")
    x = blk // 8
    y = (blk // 2) % 4
    c = blk % 2
    h = z // 2
    l = ((z + 1) // 2) % 2
    twin = h * 2 + (z + 1) % 2
    flip = 3 - z
    far_x, far_y = (x + 2) % 4, (y + 2) % 4

    def dev(xx, yy, cc, zz):
        return ((xx * 4 + yy) * 2 + cc, zz)

    right = (dev(x, (y + 1) % 4, c, z), dev((x + 1) % 4, y, c, z))
    left = (dev(x, (y + 3) % 4, c, z), dev((x + 3) % 4, y, c, z))
    other = dev(x, y, 1 - c, z)
    gathered = (qg, pg)
    pos = (y, x)

    def remote(src, dst, ssem, rsem, device):
        return pltpu.make_async_remote_copy(
            src_ref=src, dst_ref=dst, send_sem=ssem, recv_sem=rsem, device_id=device, device_id_type=MESH
        )

    def arrived(dst, sem):
        pltpu.make_async_copy(dst, dst, sem).wait()

    barrier = pltpu.get_barrier_semaphore()
    peers = [other]
    for device in (*right, *left):
        peers.append(device)
        peers.append((device[0] + 1 - 2 * c, device[1]))
    for dz in (1, 2, 3):
        for cc in (0, 1):
            peers.append(dev(x, y, cc, (z + dz) % 4))
    for peer in peers:
        pl.semaphore_signal(barrier, inc=1, device_id=peer, device_id_type=MESH)
    pl.semaphore_wait(barrier, len(peers))
    stat_peers = [dev(x, (y + dy) % 4, cc, zz) for dy in (2, 1, 3) for zz in (twin, z) for cc in (0, 1)]
    stat_peers += [dev(x, y, 0, twin), dev(x, y, 1, twin), other]
    loss_peers = [dev(x, y, c, flip)]
    for dx in (1, 2, 3):
        for zz in (z, flip):
            loss_peers.append(dev((x + dx) % 4, y, c, zz))

    turn = 1 - 2 * (z % 2)

    def z_of(which, slot):
        step = (turn, -turn)[which]
        return (z + 4 + (0, -step, step, 2)[slot]) % 4

    def holds(which, zz):
        return zz // 2 if which == 0 else ((zz + 1) // 2) % 2

    def cols(slot, start=0):
        return slice(start + (MC if slot == 3 else 0), start + WC)

    def member(which, zz):
        return (zz % 2, (zz + 1) % 2)[which]

    def lacks(which, one):
        return (holds(which, z) != c) & (member(which, z) == one)

    def fill(start):
        for which in (0, 1):
            for one in (0, 1):

                @pl.when(lacks(which, one))
                def _():
                    for part in (0, 1):
                        dst = (in_q, in_p)[which].at[one, :, part * WC:part * WC + MC]
                        copy = pltpu.make_async_copy(zero, dst, s_fill.at[which, part])
                        copy.start() if start else copy.wait()

    def along_z(slot, start):
        for which in (0, 1):
            zt = z_of(which, slot)

            @pl.when(holds(which, zt) == c)
            def _():
                for part in (0, 1):
                    src = (q_hbm, p_hbm)[which].at[:, cols(slot, part * WC)]
                    dst = gathered[which].at[slot, rows(pos[which]), cols(slot)]
                    copy = remote(src, dst, s1.at[which, slot, part], r1.at[which, slot], dev(x, y, part, zt))
                    if slot == 0:
                        for half in (0, 1):
                            for side, device in ((0, right[which]), (1, left[which])):
                                off = (side, 1 - side)[half] * HALF
                                direct = remote(
                                    (q_hbm, p_hbm)[which].at[off:off + HALF, cols(slot, part * WC)],
                                    gathered[which].at[slot, rows(pos[which], HALF, off), cols(slot)],
                                    s0.at[which, part, side, half], rn.at[which, slot, side, half],
                                    (device[0] - c + part, device[1]),
                                )
                                direct.start() if start else direct.wait_send()
                        if start:
                            @pl.when(c == part)
                            def _():
                                pltpu.make_async_copy(src, dst, r1.at[which, slot]).start()

                        @pl.when(c != part)
                        def _():
                            copy.start() if start else copy.wait_send()
                    else:
                        copy.start() if start else copy.wait_send()

    def to_next(slot, start):
        for which in (0, 1):
            own = gathered[which].at[slot, rows(pos[which]), cols(slot)]
            if start:
                arrived(own, r1.at[which, slot])
            for half in (0, 1):
                for side, device in ((0, right[which]), (1, left[which])):
                    part = gathered[which].at[slot, rows(pos[which], HALF, (side, 1 - side)[half] * HALF), cols(slot)]
                    copy = remote(part, part, sn.at[which, slot, side, half], rn.at[which, slot, side, half], device)
                    copy.start() if start else copy.wait_send()

    def from_next(which, slot, side, half):
        origin = (pos[which] + (3, 1)[side]) % 4
        part = gathered[which].at[slot, rows(origin, HALF, (side, 1 - side)[half] * HALF), cols(slot)]
        return part, rn.at[which, slot, side, half]

    def to_far(slot, start):
        for which in (0, 1):
            for side, device in ((0, right[which]), (1, left[which])):
                part, came = from_next(which, slot, side, 0)
                if start:
                    arrived(part, came)
                copy = remote(part, part, sf.at[which, slot, side], rf.at[which, slot, side], device)
                copy.start() if start else copy.wait_send()

    def rest_of_next(slot):
        for which in (0, 1):
            for side in (0, 1):
                arrived(*from_next(which, slot, side, 1))

    def from_far(slot):
        for which in (0, 1):
            for side in (0, 1):
                far = rows((pos[which] + 2) % 4, HALF, side * HALF)
                arrived(gathered[which].at[slot, far, cols(slot)], rf.at[which, slot, side])

    mates = [dev(x, y, c, z_of(which, 2)) for which in (0, 1)]

    def to_mate(start, steps=(0, 1, 2, 3)):
        for which in (0, 1):
            for step in steps:
                block = (pos[which] + step) % 4
                copy = remote(
                    gathered[which].at[1, rows(block), 0:MC], gathered[which].at[3, rows(block), 0:MC],
                    sm.at[which, block], rm.at[which, block], mates[which],
                )
                copy.start() if start else copy.wait_send()

    def scores(slot, block):
        part = lax.dot_general(
            pg[PAIRED[slot], rows(block), :], qg[slot], (((1,), (1,)), ((), ())), preferred_element_type=F32
        )
        if slot == 0:
            tile[rows(block), :] = part
        else:
            tile[rows(block), :] += part

    def all_scores(slot):
        pl.loop(0, 4)(lambda block: scores(slot, block))

    along_z(0, True)
    along_z(1, True)
    along_z(2, True)
    zero[...] = jnp.zeros((BR, MC), BF16)
    fill(True)
    to_far(0, True)
    to_next(1, True)
    along_z(3, True)
    to_mate(True, (0,))
    to_next(2, True)
    to_far(1, True)
    rest_of_next(1)
    to_mate(True, (1, 3))
    for which in (0, 1):
        arrived(gathered[which].at[0, rows(pos[which])], r1.at[which, 0])
    rest_of_next(0)
    from_far(0)
    to_far(2, True)
    to_next(3, True)
    all_scores(0)
    from_far(1)
    to_mate(True, (2,))
    rest_of_next(2)
    from_far(2)
    to_far(3, True)
    all_scores(1)
    all_scores(2)
    rest_of_next(3)
    from_far(3)
    for which in (0, 1):
        for block in range(4):
            arrived(gathered[which].at[3, rows(block), 0:MC], rm.at[which, block])

    def give_tile(j):
        return remote(
            tile.at[rows(2 * (1 - c) + j)], tile_in.at[pl.ds(j * BR, BR)], sst.at[j], rt.at[j], other
        )

    for j in (0, 1):
        scores(3, 2 * (1 - c) + j)
        give_tile(j).start()
    for j in (0, 1):
        scores(3, 2 * c + j)

    lane = lax.broadcasted_iota(jnp.int32, (1, TILE), 1)
    lanes = lax.broadcasted_iota(jnp.int32, (SUB, TILE), 1)
    subs = lax.broadcasted_iota(jnp.int32, (SUB, TILE), 0)
    eye = lanes - subs

    def diagonal(j):
        return jnp.where((2 * c + j == x) & (h == l), y * BR, -2 * TILE)

    def fold(op, acc, value):
        for k in range(0, SUB, 8):
            acc = op(acc, value[k:k + 8, :])
        return acc

    top = jnp.full((8, TILE), NEG, F32)
    diag = jnp.zeros((8, TILE), F32)
    for j in (0, 1):
        block = ((2 * c + j) * 4 + y) * 2 + l
        allow = None
        for yy in (3, 2, 1, 0):
            mine = (x * 4 + yy) * 2 + h
            flag = jnp.where(mine == block, 1, pairs_ref[mine, block])
            allow = jnp.full((1, TILE), flag, jnp.int32) if allow is None else jnp.where(lane < (yy + 1) * BR, flag, allow)
        allowed = jnp.broadcast_to(allow, (SUB, TILE)) == 1
        start = diagonal(j)
        arrived(tile_in.at[pl.ds(j * BR, BR)], rt.at[j])

        def first(i, carry):
            top, diag = carry
            here = rows(2 * c + j, SUB, i * SUB)
            value = (tile[here, :] + tile_in[pl.ds(pl.multiple_of(j * BR + i * SUB, SUB), SUB), :]) * SCALE
            diag = fold(jnp.add, diag, jnp.where(eye == start + i * SUB, value, 0.0))
            value = jnp.where(allowed, value, NEG)
            tile[here, :] = value
            return fold(jnp.maximum, top, value), diag

        top, diag = lax.fori_loop(0, BR // SUB, first, (top, diag))
    top = jnp.max(top, axis=0, keepdims=True)
    diag = jnp.sum(diag, axis=0, keepdims=True)

    total = jnp.zeros((8, TILE), F32)
    for j in (0, 1):

        def second(i, total):
            here = rows(2 * c + j, SUB, i * SUB)
            value = tile[here, :]
            value = jnp.where(value == NEG, 0.0, jnp.exp(value - top))
            tile[here, :] = value
            return fold(jnp.add, total, value)

        total = lax.fori_loop(0, BR // SUB, second, total)
    total = jnp.sum(total, axis=0, keepdims=True)

    def pack(row):
        parts = [row[:, k * 128:(k + 1) * 128] for k in range(TILE // 128)]
        return jnp.concatenate(parts + [jnp.zeros((1, 128), F32)], axis=0)

    def unpack(block):
        return jnp.concatenate([block[k:k + 1, :] for k in range(TILE // 128)], axis=1)

    mine = (y * 2 + l) * 2 + c
    stat[0:8, :] = pack(jnp.where(total > 0, top + jnp.log(total), NEG))
    stat[8:16, :] = pack(diag)
    stats[mine] = stat[...]
    stat_copies = [
        remote(stat, stats.at[mine], sstat.at[i], rst.at[mine], peer) for i, peer in enumerate(stat_peers)
    ]
    for copy in stat_copies:
        copy.start()
    for slot in range(16):
        pl.when(slot != mine)(lambda slot=slot: arrived(stats.at[slot], rst.at[slot]))
    highest = stats[0, 0:8, :]
    for slot in range(1, 16):
        highest = jnp.maximum(highest, stats[slot, 0:8, :])
    totals = jnp.zeros((8, 128), F32)
    positive = jnp.zeros((8, 128), F32)
    for slot in range(16):
        totals = totals + jnp.exp(stats[slot, 0:8, :] - highest)
        positive = positive + stats[slot, 8:16, :]
    log_total = highest + jnp.log(totals)
    factor = jnp.exp(top - unpack(log_total))

    def give_wp(j):
        part = wp.at[rows(2 * c + j)]
        return remote(part, part, sw.at[j], rw.at[j], other)

    for j in (0, 1):
        start = diagonal(j)

        def third(i, _):
            here = rows(2 * c + j, SUB, i * SUB)
            value = tile[here, :] * factor - jnp.where(eye == start + i * SUB, 1.0, 0.0)
            wp[here, :] = value.astype(BF16)
            return _

        lax.fori_loop(0, BR // SUB, third, 0)
        give_wp(j).start()
    my_rows = pl.ds(pl.multiple_of(c * CORE, CORE), CORE)
    wq[c] = jnp.transpose(wp[my_rows, :])

    group = x * 2 + h
    row = lax.broadcasted_iota(jnp.int32, (8, 128), 0)
    lossv[...] = jnp.full((8, 128), jnp.sum(jnp.where(row < TILE // 128, log_total - positive, 0.0)), F32)
    losses[group] = lossv[...]
    loss_copies = [
        remote(lossv, losses.at[group], sl.at[i], rl.at[group], peer) for i, peer in enumerate(loss_peers)
    ]
    for copy in loss_copies:
        copy.start()

    for j in (0, 1):
        arrived(wp.at[rows(2 * (1 - c) + j)], rw.at[j])

    def gradient(which, slot, block, span):
        if which == 1:
            return jnp.dot(wp[rows(block), :], qg[PAIRED[slot], :, span], preferred_element_type=F32)
        return jnp.dot(wq[0, rows(block), :], pg[PAIRED[slot], 0:CORE, span], preferred_element_type=F32) + jnp.dot(
            wq[1, rows(block), :], pg[PAIRED[slot], CORE:TILE, span], preferred_element_type=F32
        )

    def total_of(which, slot, block):
        part = gradient(which, slot, block, cols(slot))
        if slot == 1:
            arrived(in_m.at[which, block], rm5.at[which, block])
            part = jnp.concatenate([part[:, 0:MC] + in_m[which, block].astype(F32), part[:, MC:WC]], axis=1)
        return part

    def far_copy(which, slot, side):
        return remote(
            st_f.at[which, slot, pl.ds(side * HALF, HALF), cols(slot)], in_f.at[which, slot, side, :, cols(slot)],
            sf5.at[which, slot, side], rf5.at[which, slot, side], (right, left)[side][which],
        )

    def next_copy(which, slot, side, half):
        off = (1 - side, side)[half] * HALF
        return remote(
            st_n.at[which, slot, side, pl.ds(off, HALF), cols(slot)],
            in_n.at[which, slot, side, pl.ds(off, HALF), cols(slot)],
            sn5.at[which, slot, side, half], rn5.at[which, slot, side, half], (right, left)[side][which],
        )

    def mate_copy(which, block):
        return remote(
            st_m.at[which, block], in_m.at[which, block], sm5.at[which, block], rm5.at[which, block], mates[which]
        )

    def z_copy(which, slot):
        owner = holds(which, z)
        first = c * WC + (MC if slot == 3 else 0)
        span = pl.ds(pl.multiple_of(first, 128), WC - MC if slot == 3 else WC)
        dst = (in_q, in_p)[which].at[member(which, z), :, span]
        return owner, dst, remote(
            st_z.at[which, slot, :, cols(slot)], dst, sz.at[which, slot], rz.at[which, member(which, z), c],
            dev(x, y, owner, z_of(which, slot)),
        )

    def send_mate():
        for which in (1, 0):
            for step in (2, 1, 3, 0):
                block = (pos[which] + step) % 4
                st_m[which, block] = gradient(which, 3, block, slice(0, MC)).astype(BF16)
                mate_copy(which, block).start()

    def send_far(slot):
        for which in (1, 0):
            if which == 0 and slot == 2:
                wq[1 - c] = jnp.transpose(wp[pl.ds(pl.multiple_of((1 - c) * CORE, CORE), CORE), :])
            st_f[which, slot, :, cols(slot)] = total_of(which, slot, (pos[which] + 2) % 4).astype(BF16)
            for side in (0, 1):
                far_copy(which, slot, side).start()

    def send_next(slot):
        for which in (1, 0):
            for side in (0, 1):
                part = total_of(which, slot, (pos[which] + (1, 3)[side]) % 4)
                add, keep = slice(side * HALF, (side + 1) * HALF), slice((1 - side) * HALF, (2 - side) * HALF)
                st_n[which, slot, side, keep, cols(slot)] = part[keep].astype(BF16)
                next_copy(which, slot, side, 0).start()
                arrived(in_f.at[which, slot, side, :, cols(slot)], rf5.at[which, slot, side])
                st_n[which, slot, side, add, cols(slot)] = (
                    part[add] + in_f[which, slot, side, :, cols(slot)].astype(F32)
                ).astype(BF16)
                next_copy(which, slot, side, 1).start()

    def send_home(slot):
        for which in (1, 0):
            part = total_of(which, slot, pos[which])
            for side in (0, 1):
                for half in (0, 1):
                    off = (1 - side, side)[half] * HALF
                    arrived(in_n.at[which, slot, side, pl.ds(off, HALF), cols(slot)], rn5.at[which, slot, side, half])
                part = part + in_n[which, slot, side, :, cols(slot)].astype(F32)
            st_z[which, slot, :, cols(slot)] = part.astype(BF16)
            owner, dst, copy = z_copy(which, slot)
            if slot == 0:

                @pl.when(owner == c)
                def _():
                    pltpu.make_async_copy(st_z.at[which, slot], dst, rz.at[which, member(which, z), c]).start()

                @pl.when(owner != c)
                def _():
                    copy.start()
            else:
                copy.start()

    send_far(2)
    send_far(3)
    send_far(0)
    send_mate()
    send_next(2)
    send_next(3)
    send_far(1)
    send_home(2)
    send_next(1)
    send_home(3)
    send_next(0)
    send_home(1)
    send_home(0)

    to_mate(False)
    for slot in range(4):
        along_z(slot, False)
        if slot > 0:
            to_next(slot, False)
        to_far(slot, False)
    for j in (0, 1):
        give_tile(j).wait_send()
    for copy in stat_copies:
        copy.wait_send()
    for j in (0, 1):
        give_wp(j).wait_send()
    for copy in loss_copies:
        copy.wait_send()
    for which in (0, 1):
        for slot in range(4):
            mate_copy(which, slot).wait_send()
            for side in (0, 1):
                far_copy(which, slot, side).wait_send()
                for half in (0, 1):
                    next_copy(which, slot, side, half).wait_send()

    for slot in range(8):
        pl.when(slot != group)(lambda slot=slot: arrived(losses.at[slot], rl.at[slot]))
    loss = losses[0]
    for slot in range(1, 8):
        loss = loss + losses[slot]
    loss_ref[0, 0] = loss[0, 0] / (32 * BR)

    for which in (0, 1):
        for part in (0, 1):
            for one in (0, 1):
                whole = (in_q, in_p)[which].at[one, :, part * WC:(part + 1) * WC]
                rest = (in_q, in_p)[which].at[one, :, cols(3, part * WC)]
                half = lacks(which, one)
                pl.when(half)(lambda rest=rest, one=one, part=part, which=which: arrived(rest, rz.at[which, one, part]))
                pl.when(jnp.logical_not(half))(
                    lambda whole=whole, one=one, part=part, which=which: arrived(whole, rz.at[which, one, part])
                )
    fill(False)
    for which in (0, 1):
        for slot in range(4):
            owner, _, copy = z_copy(which, slot)
            if slot == 0:
                pl.when(owner != c)(lambda copy=copy: copy.wait_send())
            else:
                copy.wait_send()


def body(queries, passages, pairs):
    dma = pltpu.SemaphoreType.DMA
    loss, in_q, in_p = pl.pallas_call(
        kernel,
        out_shape=(
            jax.ShapeDtypeStruct((1, 1), F32),
            jax.ShapeDtypeStruct((2, *queries.shape), BF16),
            jax.ShapeDtypeStruct((2, *passages.shape), BF16),
        ),
        in_specs=[
            pl.BlockSpec(memory_space=pl.ANY),
            pl.BlockSpec(memory_space=pl.ANY),
            pl.BlockSpec(memory_space=pltpu.SMEM),
        ],
        out_specs=(
            pl.BlockSpec(memory_space=pltpu.SMEM),
            pl.BlockSpec(memory_space=pl.ANY),
            pl.BlockSpec(memory_space=pl.ANY),
        ),
        scratch_shapes=[
            pltpu.VMEM((4, TILE, WC), BF16),
            pltpu.VMEM((4, TILE, WC), BF16),
            pltpu.VMEM((TILE, TILE), F32),
            pltpu.VMEM((CORE, TILE), F32),
            pltpu.VMEM((TILE, TILE), BF16),
            pltpu.VMEM((2, TILE, CORE), BF16),
            pltpu.VMEM((2, 4, BR, WC), BF16),
            pltpu.VMEM((2, 4, 2, HALF, WC), BF16),
            pltpu.VMEM((2, 4, 2, BR, WC), BF16),
            pltpu.VMEM((2, 4, 2, BR, WC), BF16),
            pltpu.VMEM((2, 4, BR, WC), BF16),
            pltpu.VMEM((2, 4, BR, MC), BF16),
            pltpu.VMEM((2, 4, BR, MC), BF16),
            pltpu.VMEM((BR, MC), BF16),
            pltpu.VMEM((16, 128), F32),
            pltpu.VMEM((16, 16, 128), F32),
            pltpu.VMEM((8, 128), F32),
            pltpu.VMEM((8, 8, 128), F32),
            dma((2, 4)), dma((2, 4, 2)), dma((2, 2, 2, 2)),
            dma((2, 4, 2, 2)), dma((2, 4, 2, 2)),
            dma((2, 4, 2)), dma((2, 4, 2)),
            dma((2,)), dma((2,)),
            dma((16,)), dma((15,)),
            dma((2,)), dma((2,)),
            dma((2, 4, 2)), dma((2, 4, 2)),
            dma((2, 4, 2, 2)), dma((2, 4, 2, 2)),
            dma((2, 2, 2)), dma((2, 4)),
            dma((8,)), dma((7,)),
            dma((2, 4)), dma((2, 4)),
            dma((2, 4)), dma((2, 4)),
            dma((2, 2)),
        ],
        compiler_params=pltpu.CompilerParams(
            collective_id=0, has_side_effects=True, vmem_limit_bytes=56 * 2**20
        ),
    )(queries, passages, pairs)
    grads = [(pair[0].astype(F32) + pair[1].astype(F32)).astype(BF16) for pair in (in_q, in_p)]
    return loss.reshape(()), *grads


def solution(mesh):
    return jax.shard_map(
        body,
        mesh=mesh,
        in_specs=(P("blk", "wid"), P("blk", "wid"), P()),
        out_specs=(P(), P("blk", "wid"), P("blk", "wid")),
        check_vma=False,
    )
```
